32 devices in a mesh: ctx: 8 (over z, y), head: 4 (over x, core).
Axes of the slice: x: 2, y: 2, z: 4, core: 2. Of those that a mesh axis runs over, the one named last changes fastest.
Arguments:
- queries: bfloat16 [1024, 64, 576], P('ctx', 'head'), may hold values from -100 to 100
- latent_cache: bfloat16 [16, 36864], P('ctx'), may hold values from -6 to 6
- selected: int32 [16, 8], P('ctx'), may hold values from -1 to 15, as said below
- value_weight: bfloat16 [64, 512, 128], P('head'), may hold values from -0.25 to 0.25
Outputs:
- attended: bfloat16 [1024, 8192], P(('ctx', 'head'))
The draws below stay inside these ranges and needn't reach their ends.
Inputs may be any that keep to these rules, and one draw needn't show every extreme that they name: `selected`: row b lists distinct key blocks: its first entry is b itself, the others lie below b; where b + 1 < 8 the row holds all of 0 to b and its remaining slots are -1.
All inputs are finite; a program needn't handle non-finite values.
Results may differ from the reference program's by a relative error of at most 0.011.
Values may be sent and summed in bfloat16 or wider, within the bound.
A program may use at most 64 MiB of HBM per device.

```python
import jax
import jax.numpy as jnp
from jax import lax

DC = 512
DR = 64
DV = 128
HEADS = 64
KBLK = 64
SEL = 8
NBLK = 16
TOKENS = 1024


def build_pair(key):
    cache_key = jax.random.fold_in(key, 11)
    query_key = jax.random.fold_in(key, 12)
    latent_width = DC + DR
    latent_rows = jnp.clip(jax.random.normal(cache_key, (TOKENS, latent_width), jnp.float32), -6.0, 6.0)
    query_vals = jnp.clip(jax.random.normal(query_key, (TOKENS, HEADS, latent_width), jnp.float32), -6.0, 6.0)
    return (latent_rows, query_vals)


def draw_queries(key, part):
    latent_rows, query_vals = build_pair(key)
    return query_vals.astype(jnp.bfloat16)


def draw_latent_cache(key, part):
    latent_rows, query_vals = build_pair(key)
    return latent_rows.reshape(NBLK, KBLK * (DC + DR)).astype(jnp.bfloat16)


def draw_selected(key, part):
    row_index = jnp.arange(NBLK, dtype=jnp.int32)[:, None]
    col_index = jnp.arange(NBLK, dtype=jnp.int32)[None, :]
    jitter = jax.random.randint(jax.random.fold_in(key, 21), (NBLK, NBLK), 0, 2 ** 20, dtype=jnp.int32)
    ranking = jnp.where(col_index < row_index, jitter * NBLK + col_index, -1 - col_index)
    ranked = lax.top_k(ranking, SEL - 1)[0]
    picked = jnp.where(ranked >= 0, ranked % NBLK, -1)
    own_block = jnp.arange(NBLK, dtype=jnp.int32)[:, None]
    return jnp.concatenate([own_block, picked.astype(jnp.int32)], axis=1).astype(jnp.int32)


def block_scale(key, shape, shards, smallest, high):
    loudness = 1.0
    for dim, parts in shards:
        steps = jax.random.uniform(jax.random.fold_in(jax.random.fold_in(key, 6), dim), (parts,), jnp.float32, smallest / len(shards), high / len(shards))
        loudness = loudness * jnp.repeat(jnp.exp(steps), shape[dim] // parts).reshape((-1,) + (1,) * (len(shape) - 1 - dim))
    return loudness


def bell_draw(own_key, shape, width, bound, shards=(), kind=jnp.bfloat16):
    result = jax.random.normal(own_key, shape, jnp.float32) * width
    if len(shards) > 0:
        result = block_scale(own_key, shape, shards, -0.22, 0.18) * result
    return jnp.clip(result, min=-bound, max=bound).astype(kind)


def setup_inputs(seed: int = 0) -> dict:
    key_of = jax.random.split(jax.random.key(seed), 5)
    queries = draw_queries(jax.random.fold_in(key_of[4], 71), 0)
    latent_cache = draw_latent_cache(jax.random.fold_in(key_of[4], 71), 0)
    selected = draw_selected(jax.random.fold_in(key_of[4], 71), 0)
    value_weight = bell_draw(key_of[3], (HEADS, DC, DV), DC ** -0.5, 0.25, ((0, 4),))
    return {"queries": queries, "latent_cache": latent_cache, "selected": selected, "value_weight": value_weight}


def reference(queries, latent_cache, selected, value_weight):
    latent_width = DC + DR
    score_scale = (DV + DR) ** -0.5
    blocked = latent_cache.reshape(NBLK, KBLK, latent_width)
    offsets = jnp.arange(KBLK, dtype=jnp.int32)

    def one_block(block_index):
        chosen_ids = selected[block_index]
        valid_slot = chosen_ids >= 0
        clipped = jnp.maximum(chosen_ids, 0).astype(jnp.int32)
        key_rows = blocked[clipped].reshape(SEL * KBLK, latent_width)
        key_place = (clipped[:, None] * KBLK + offsets[None, :]).reshape(SEL * KBLK)
        key_valid = jnp.repeat(valid_slot, KBLK)
        query_rows = lax.dynamic_slice_in_dim(queries, (block_index * KBLK).astype(jnp.int32), KBLK, 0)
        query_place = block_index * KBLK + offsets
        scores = jnp.einsum("qhc,kc->hqk", query_rows.astype(jnp.float32), key_rows.astype(jnp.float32)) * score_scale
        allowed = key_valid[None, None, :] & (key_place[None, None, :] <= query_place[None, :, None])
        scores = jnp.where(allowed, scores, -1e30)
        largest = jnp.max(scores, axis=2, keepdims=True)
        powered = jnp.exp(scores - largest)
        weights = (powered / jnp.sum(powered, axis=2, keepdims=True)).astype(jnp.bfloat16)
        mixed_latent = jnp.einsum("hqk,kc->qhc", weights.astype(jnp.float32), key_rows[:, :DC].astype(jnp.float32)).astype(jnp.bfloat16)
        expanded = jnp.einsum("qhc,hcv->qhv", mixed_latent.astype(jnp.float32), value_weight.astype(jnp.float32))
        return expanded.astype(jnp.bfloat16).reshape(KBLK, HEADS * DV)

    per_block = lax.map(one_block, jnp.arange(NBLK, dtype=jnp.int32))
    return per_block.reshape(TOKENS, HEADS * DV)
```

```python
import functools
import math

import jax
import jax.numpy as jnp
from jax import lax
from jax.experimental import pallas as pl
from jax.experimental.pallas import tpu as pltpu
from jax.sharding import PartitionSpec as P

DC = 512
DR = 64
DV = 128
KBLK = 64
SEL = 8
GROUPS = 4
MESH = pl.DeviceIdType.MESH
FAR = 1 << 30


def kernel(
    n_ctx, n_head, heads,
    sel_ref, own_ref, q_hbm, w_hbm, out_ref,
    keys, kbuf, q_ref, q_blocks, w_ref, stage,
    load_sem, s1, r1, s2, r2, s3, r3, s4, r4, s_out, r_out, l_out,
):
    c = lax.axis_index("ctx")
    h = lax.axis_index("head")
    x, core = h // 2, h % 2
    h_core = 2 * x + (1 - core)
    h_x = 2 * (1 - x) + core
    h_diag = 2 * (1 - x) + (1 - core)
    own_rows = own_ref.shape[0]
    blocks = own_rows // KBLK
    part = own_rows // n_head

    load_q = pltpu.make_async_copy(q_hbm, q_ref, load_sem.at[0])
    load_w = pltpu.make_async_copy(w_hbm, w_ref, load_sem.at[1])
    load_q.start()
    load_w.start()

    barrier = pltpu.get_barrier_semaphore()
    for peer in (h_core, h_x, h_diag):
        pl.semaphore_signal(barrier, inc=1, device_id=(c, peer), device_id_type=MESH)

    @pl.loop(0, c)
    def _(lower):
        pl.semaphore_signal(barrier, inc=1, device_id=(lower, h), device_id_type=MESH)

    pl.semaphore_wait(barrier, 3 + n_ctx - 1 - c)

    def piece(source, quarter):
        row = quarter * part
        start = pl.multiple_of(row % KBLK, part)
        return keys.at[source * blocks + row // KBLK, pl.ds(start, part), :]

    def first_copy(source, target):
        return pltpu.make_async_remote_copy(
            src_ref=own_ref.at[pl.ds(pl.multiple_of(h * part, part), part), :],
            dst_ref=piece(source, h),
            send_sem=s1.at[target], recv_sem=r1.at[source],
            device_id=(target, h), device_id_type=MESH,
        )

    def relay(source, quarter, peer, send, recv):
        return pltpu.make_async_remote_copy(
            src_ref=piece(source, quarter), dst_ref=piece(source, quarter),
            send_sem=send.at[source], recv_sem=recv.at[source],
            device_id=(c, peer), device_id_type=MESH,
        )

    @pl.loop(0, n_ctx - 1 - c)
    def _(step):
        first_copy(c, n_ctx - 1 - step).start()

    for block in range(blocks):
        keys[c * blocks + block] = own_ref[block * KBLK:(block + 1) * KBLK, :]

    @pl.loop(0, c + 1)
    def _(step):
        @pl.when(step < c)
        def _():
            source = c - 1 - step
            first_copy(source, c).wait_recv()
            relay(source, h, h_x, s2, r2).start()
            relay(source, h, h_core, s3, r3).start()

        @pl.when(step > 0)
        def _():
            source = c - step
            relay(source, h_x, h_x, s2, r2).wait_recv()
            relay(source, h_x, h_core, s4, r4).start()

    load_q.wait()
    for pair in range(heads // 2):
        group, slot = divmod(pair, heads // (2 * GROUPS))
        lanes = slice(slot * 2 * KBLK, (slot + 1) * 2 * KBLK)
        first, second = q_ref[2 * pair], q_ref[2 * pair + 1]
        q_blocks[0, group, :, lanes] = jnp.concatenate([first[:, :KBLK], second[:, :KBLK]], axis=1)
        q_blocks[1, group, :, lanes] = jnp.concatenate([first[:, KBLK:], second[:, KBLK:]], axis=1)
    load_w.wait()

    @pl.loop(0, c)
    def _(step):
        source = c - 1 - step
        relay(source, h_core, h_core, s3, r3).wait_recv()
        relay(source, h_diag, h_core, s4, r4).wait_recv()

    factor = (DV + DR) ** (-0.5) * math.log2(math.e)
    key_row = lax.broadcasted_iota(jnp.int32, (SEL * KBLK, 1), 0)
    per_group = heads // GROUPS
    width = per_group * DV
    columns = per_group * KBLK
    token = lax.broadcasted_iota(jnp.int32, (1, columns), 1) % KBLK

    def out_copy(group, target, relation):
        return pltpu.make_async_remote_copy(
            src_ref=stage.at[target, :, pl.ds(group * width, width)],
            dst_ref=out_ref.at[:, pl.ds(pl.multiple_of(h * (heads * DV) + group * width, width), width)],
            send_sem=s_out.at[relation, group], recv_sem=r_out.at[relation, group],
            device_id=(c, target), device_id_type=MESH,
        )

    def out_local(group):
        return pltpu.make_async_copy(
            stage.at[h, :, pl.ds(group * width, width)],
            out_ref.at[:, pl.ds(pl.multiple_of(h * (heads * DV) + group * width, width), width)],
            l_out.at[group],
        )

    half = KBLK // 2
    for turn in range(2):
        position = (1 - x) if turn == 0 else x
        key_block = jnp.zeros((SEL * KBLK, 1), jnp.int32)
        for slot in range(SEL):
            chosen = sel_ref[position, slot]
            kbuf[slot * KBLK:(slot + 1) * KBLK, :] = keys[jnp.maximum(chosen, 0)]
            key_block = jnp.where(key_row // KBLK == slot, chosen, key_block)
        key_place = jnp.where(key_block < 0, FAR, key_block * KBLK + key_row % KBLK)

        query_place = token + (c * blocks + position) * KBLK
        for group in range(GROUPS):
            query = q_blocks[position, group]
            scores = jnp.dot(kbuf[...], query, preferred_element_type=jnp.float32)
            scores = jnp.where(key_place <= query_place, scores, -1e30)
            largest = jnp.max(scores, axis=0, keepdims=True)
            powered = jnp.exp2((scores - largest) * factor)
            total = jnp.sum(powered, axis=0, keepdims=True)
            weights = (powered * (1.0 / total)).astype(jnp.bfloat16)
            latent = jnp.dot(
                weights.T, kbuf[:, :DC], preferred_element_type=jnp.float32
            ).astype(jnp.bfloat16)
            for inner in range(per_group):
                head = group * per_group + inner
                value = jnp.dot(
                    latent[inner * KBLK:(inner + 1) * KBLK], w_ref[head], preferred_element_type=jnp.float32
                ).astype(jnp.bfloat16)
                stage[2 * position, :, head * DV:(head + 1) * DV] = value[:half]
                stage[2 * position + 1, :, head * DV:(head + 1) * DV] = value[half:]
            if turn == 0:
                out_copy(group, h_x, 0).start()
                out_copy(group, h_diag, 1).start()
            else:
                out_copy(group, h_core, 2).start()
                out_local(group).start()

    for group in range(GROUPS):
        out_local(group).wait()
        for relation, peer in enumerate((h_x, h_diag, h_core)):
            out_copy(group, peer, relation).wait()

    @pl.loop(0, n_ctx - 1 - c)
    def _(step):
        first_copy(c, n_ctx - 1 - step).wait_send()

    @pl.loop(0, c)
    def _(source):
        relay(source, h, h_x, s2, r2).wait_send()
        relay(source, h, h_core, s3, r3).wait_send()
        relay(source, h_x, h_core, s4, r4).wait_send()


def per_device(queries, latent_cache, selected, value_weight):
    n_ctx, n_head = lax.axis_size("ctx"), lax.axis_size("head")
    width = DC + DR
    tokens, heads = queries.shape[:2]
    own = latent_cache.reshape(tokens, width)
    by_head = queries.transpose(1, 2, 0)
    part = tokens // n_head
    dma = pltpu.SemaphoreType.DMA
    return pl.pallas_call(
        functools.partial(kernel, n_ctx, n_head, heads),
        out_shape=jax.ShapeDtypeStruct((part, n_head * heads * DV), jnp.bfloat16),
        in_specs=[
            pl.BlockSpec(memory_space=pltpu.SMEM),
            pl.BlockSpec(memory_space=pltpu.VMEM),
            pl.BlockSpec(memory_space=pl.ANY),
            pl.BlockSpec(memory_space=pl.ANY),
        ],
        out_specs=pl.BlockSpec(memory_space=pl.ANY),
        scratch_shapes=[
            pltpu.VMEM((n_ctx * tokens // KBLK, KBLK, width), jnp.bfloat16),
            pltpu.VMEM((SEL * KBLK, width), jnp.bfloat16),
            pltpu.VMEM((heads, width, tokens), jnp.bfloat16),
            pltpu.VMEM((tokens // KBLK, GROUPS, width, heads // GROUPS * KBLK), jnp.bfloat16),
            pltpu.VMEM((heads, DC, DV), jnp.bfloat16),
            pltpu.VMEM((n_head, part, heads * DV), jnp.bfloat16),
            dma((2,)),
            dma((n_ctx,)), dma((n_ctx,)),
            dma((n_ctx,)), dma((n_ctx,)),
            dma((n_ctx,)), dma((n_ctx,)),
            dma((n_ctx,)), dma((n_ctx,)),
            dma((3, GROUPS)), dma((3, GROUPS)), dma((GROUPS,)),
        ],
        compiler_params=pltpu.CompilerParams(
            collective_id=0, has_side_effects=True, vmem_limit_bytes=52 * 1024 * 1024
        ),
    )(selected, own, by_head, value_weight)


def solution(mesh):
    in_specs = (P("ctx", "head", None), P("ctx", None), P("ctx", None), P("head", None, None))
    out_specs = P(("ctx", "head"), None)
    return jax.shard_map(
        per_device, mesh=mesh, in_specs=in_specs, out_specs=out_specs, check_vma=False
    )
```

```python
import functools
import math

import jax
import jax.numpy as jnp
from jax import lax
from jax.experimental import pallas as pl
from jax.experimental.pallas import tpu as pltpu
from jax.sharding import PartitionSpec as P

DC = 512
DR = 64
DV = 128
KBLK = 64
SEL = 8
GROUPS = 4
LAG_RELAY = 2
LAG_SCORE = 4
DENSE_BLOCKS = 32
MESH = pl.DeviceIdType.MESH
FAR = 1 << 30


def kernel(
    n_ctx, n_head, heads, dense,
    sel_hbm, own_ref, q_hbm, w_hbm, out_ref,
    sel_ref, keys, kbuf, q_ref, q_blocks, scored, w_ref, stage,
    load_sem, s1, r1, s2, r2, s3, r3, s4, r4, s_out, r_out, l_out,
):
    c = lax.axis_index("ctx")
    h = lax.axis_index("head")
    x, core = h // 2, h % 2
    h_core = 2 * x + (1 - core)
    h_x = 2 * (1 - x) + core
    h_diag = 2 * (1 - x) + (1 - core)
    own_rows = own_ref.shape[0]
    blocks = own_rows // KBLK
    part = own_rows // n_head

    load_q = pltpu.make_async_copy(q_hbm, q_ref, load_sem.at[0])
    load_w = pltpu.make_async_copy(w_hbm, w_ref, load_sem.at[1])
    load_sel = pltpu.make_async_copy(sel_hbm, sel_ref, load_sem.at[2])
    load_q.start()
    load_sel.start()
    load_w.start()

    barrier = pltpu.get_barrier_semaphore()
    for peer in (h_core, h_x, h_diag):
        pl.semaphore_signal(barrier, inc=1, device_id=(c, peer), device_id_type=MESH)

    @pl.loop(0, c)
    def _(lower):
        pl.semaphore_signal(barrier, inc=1, device_id=(lower, h), device_id_type=MESH)

    pl.semaphore_wait(barrier, 3 + n_ctx - 1 - c)

    def piece(source, quarter):
        row = quarter * part
        start = pl.multiple_of(row % KBLK, part)
        return keys.at[source * blocks + row // KBLK, pl.ds(start, part), :]

    def first_copy(source, target):
        return pltpu.make_async_remote_copy(
            src_ref=own_ref.at[pl.ds(pl.multiple_of(h * part, part), part), :],
            dst_ref=piece(source, h),
            send_sem=s1.at[target], recv_sem=r1.at[source],
            device_id=(target, h), device_id_type=MESH,
        )

    def relay(source, quarter, peer, send, recv):
        return pltpu.make_async_remote_copy(
            src_ref=piece(source, quarter), dst_ref=piece(source, quarter),
            send_sem=send.at[source], recv_sem=recv.at[source],
            device_id=(c, peer), device_id_type=MESH,
        )

    @pl.loop(0, n_ctx - 1 - c)
    def _(step):
        first_copy(c, n_ctx - 1 - step).start()

    for block in range(blocks):
        keys[c * blocks + block] = own_ref[block * KBLK:(block + 1) * KBLK, :]

    load_q.wait()
    per_group = heads // GROUPS
    columns = per_group * KBLK
    for pair in range(heads // 2):
        group, slot = divmod(pair, heads // (2 * GROUPS))
        lanes = slice(slot * 2 * KBLK, (slot + 1) * 2 * KBLK)
        first, second = q_ref[2 * pair], q_ref[2 * pair + 1]
        q_blocks[0, group, :, lanes] = jnp.concatenate([first[:, :KBLK], second[:, :KBLK]], axis=1)
        q_blocks[1, group, :, lanes] = jnp.concatenate([first[:, KBLK:], second[:, KBLK:]], axis=1)

    def score_source(source):
        rows = jnp.concatenate([keys[source * blocks + block] for block in range(blocks)], axis=0)
        for position in range(2):
            for group in range(GROUPS):
                result = jnp.dot(rows, q_blocks[position, group], preferred_element_type=jnp.float32)
                for block in range(blocks):
                    scored[source * blocks + block, position, group] = result[block * KBLK:(block + 1) * KBLK]

    if dense:
        score_source(c)

    @pl.loop(0, c + LAG_SCORE)
    def _(step):
        @pl.when(step < c)
        def _():
            source = c - 1 - step
            first_copy(source, c).wait_recv()
            relay(source, h, h_x, s2, r2).start()
            relay(source, h, h_core, s3, r3).start()

        @pl.when((step >= LAG_RELAY) & (step < c + LAG_RELAY))
        def _():
            source = c - 1 - (step - LAG_RELAY)
            relay(source, h_x, h_x, s2, r2).wait_recv()
            relay(source, h_x, h_core, s4, r4).start()

        @pl.when(step >= LAG_SCORE)
        def _():
            source = c - 1 - (step - LAG_SCORE)
            relay(source, h_core, h_core, s3, r3).wait_recv()
            relay(source, h_diag, h_core, s4, r4).wait_recv()
            if dense:
                score_source(source)

    load_w.wait()
    load_sel.wait()

    factor = (DV + DR) ** (-0.5) * math.log2(math.e)
    key_row = lax.broadcasted_iota(jnp.int32, (SEL * KBLK, 1), 0)
    width = per_group * DV
    token = lax.broadcasted_iota(jnp.int32, (1, columns), 1) % KBLK

    def out_copy(group, target, relation):
        return pltpu.make_async_remote_copy(
            src_ref=stage.at[target, :, pl.ds(group * width, width)],
            dst_ref=out_ref.at[:, pl.ds(pl.multiple_of(h * (heads * DV) + group * width, width), width)],
            send_sem=s_out.at[relation, group], recv_sem=r_out.at[relation, group],
            device_id=(c, target), device_id_type=MESH,
        )

    def out_local(group):
        return pltpu.make_async_copy(
            stage.at[h, :, pl.ds(group * width, width)],
            out_ref.at[:, pl.ds(pl.multiple_of(h * (heads * DV) + group * width, width), width)],
            l_out.at[group],
        )

    half = KBLK // 2

    def slots_of(position):
        chosen = [sel_ref[position, slot] for slot in range(SEL)]
        return chosen, [jnp.maximum(one, 0) for one in chosen]

    def weigh(position, group):
        chosen, entry = slots_of(position)
        key_block = jnp.full((SEL * KBLK, 1), chosen[0], jnp.int32)
        for slot in range(1, SEL):
            key_block = jnp.where(key_row // KBLK == slot, chosen[slot], key_block)
        key_place = jnp.where(key_block < 0, FAR, key_block * KBLK + key_row % KBLK)
        query_place = token + (c * blocks + position) * KBLK
        if dense:
            scores = jnp.concatenate([scored[one, position, group] for one in entry], axis=0)
        else:
            rows = jnp.concatenate([keys[one] for one in entry], axis=0)
            scores = jnp.dot(rows, q_blocks[position, group], preferred_element_type=jnp.float32)
        scores = jnp.where(key_place <= query_place, scores, -1e30)
        largest = jnp.max(scores, axis=0, keepdims=True)
        powered = jnp.exp2((scores - largest) * factor)
        total = jnp.sum(powered, axis=0, keepdims=True)
        return (powered * (1.0 / total)).astype(jnp.bfloat16).T

    def finish(turn, position, group, weights):
        latent = jnp.dot(weights, kbuf[turn], preferred_element_type=jnp.float32).astype(jnp.bfloat16)
        for inner in range(per_group):
            head = group * per_group + inner
            value = jnp.dot(
                latent[inner * KBLK:(inner + 1) * KBLK], w_ref[head], preferred_element_type=jnp.float32
            ).astype(jnp.bfloat16)
            stage[2 * position, :, head * DV:(head + 1) * DV] = value[:half]
            stage[2 * position + 1, :, head * DV:(head + 1) * DV] = value[half:]

    def send(turn, group):
        if turn == 0:
            out_copy(group, h_x, 0).start()
            out_copy(group, h_diag, 1).start()
        else:
            out_copy(group, h_core, 2).start()
            out_local(group).start()

    order = [(turn, (1 - x) if turn == 0 else x, group) for turn in range(2) for group in range(GROUPS)]
    for turn in range(2):
        _, entry = slots_of((1 - x) if turn == 0 else x)
        for slot in range(SEL):
            kbuf[turn, slot * KBLK:(slot + 1) * KBLK, :] = keys[entry[slot], :, :DC]
    weights = weigh(order[0][1], order[0][2])
    for number, (turn, position, group) in enumerate(order):
        after = None
        if number + 1 < len(order):
            after = weigh(order[number + 1][1], order[number + 1][2])
        finish(turn, position, group, weights)
        send(turn, group)
        weights = after

    for group in range(GROUPS):
        out_local(group).wait()
        for relation, peer in enumerate((h_x, h_diag, h_core)):
            out_copy(group, peer, relation).wait()

    @pl.loop(0, n_ctx - 1 - c)
    def _(step):
        first_copy(c, n_ctx - 1 - step).wait_send()

    @pl.loop(0, c)
    def _(source):
        relay(source, h, h_x, s2, r2).wait_send()
        relay(source, h, h_core, s3, r3).wait_send()
        relay(source, h_x, h_core, s4, r4).wait_send()


def per_device(queries, latent_cache, selected, value_weight):
    n_ctx, n_head = lax.axis_size("ctx"), lax.axis_size("head")
    width = DC + DR
    tokens, heads = queries.shape[:2]
    own = latent_cache.reshape(tokens, width)
    by_head = queries.transpose(1, 2, 0)
    part = tokens // n_head
    n_blocks = n_ctx * tokens // KBLK
    dense = n_blocks <= DENSE_BLOCKS
    scored_blocks = n_blocks if dense else 1
    dma = pltpu.SemaphoreType.DMA
    return pl.pallas_call(
        functools.partial(kernel, n_ctx, n_head, heads, dense),
        out_shape=jax.ShapeDtypeStruct((part, n_head * heads * DV), jnp.bfloat16),
        in_specs=[
            pl.BlockSpec(memory_space=pltpu.HBM),
            pl.BlockSpec(memory_space=pltpu.VMEM),
            pl.BlockSpec(memory_space=pl.ANY),
            pl.BlockSpec(memory_space=pl.ANY),
        ],
        out_specs=pl.BlockSpec(memory_space=pl.ANY),
        scratch_shapes=[
            pltpu.SMEM(selected.shape, jnp.int32),
            pltpu.VMEM((n_ctx * tokens // KBLK, KBLK, width), jnp.bfloat16),
            pltpu.VMEM((2, SEL * KBLK, DC), jnp.bfloat16),
            pltpu.VMEM((heads, width, tokens), jnp.bfloat16),
            pltpu.VMEM((tokens // KBLK, GROUPS, width, heads // GROUPS * KBLK), jnp.bfloat16),
            pltpu.VMEM((scored_blocks, 2, GROUPS, KBLK, heads // GROUPS * KBLK), jnp.float32),
            pltpu.VMEM((heads, DC, DV), jnp.bfloat16),
            pltpu.VMEM((n_head, part, heads * DV), jnp.bfloat16),
            dma((3,)),
            dma((n_ctx,)), dma((n_ctx,)),
            dma((n_ctx,)), dma((n_ctx,)),
            dma((n_ctx,)), dma((n_ctx,)),
            dma((n_ctx,)), dma((n_ctx,)),
            dma((3, GROUPS)), dma((3, GROUPS)), dma((GROUPS,)),
        ],
        compiler_params=pltpu.CompilerParams(
            collective_id=0, has_side_effects=True, vmem_limit_bytes=52 * 1024 * 1024
        ),
    )(selected, own, by_head, value_weight)


def solution(mesh):
    in_specs = (P("ctx", "head", None), P("ctx", None), P("ctx", None), P("head", None, None))
    out_specs = P(("ctx", "head"), None)
    return jax.shard_map(
        per_device, mesh=mesh, in_specs=in_specs, out_specs=out_specs, check_vma=False
    )
```

```python
import functools
import math

import jax
import jax.numpy as jnp
from jax import lax
from jax.experimental import pallas as pl
from jax.experimental.pallas import tpu as pltpu
from jax.sharding import PartitionSpec as P

DC = 512
DR = 64
DV = 128
KBLK = 64
SEL = 8
GROUPS = 4
DENSE_BLOCKS = 32
MESH = pl.DeviceIdType.MESH
FAR = 1 << 30


def kernel(
    n_ctx, n_head, heads, dense,
    sel_hbm, own_ref, q_hbm, w_hbm, out_ref,
    sel_ref, keys, kbuf, q_ref, q_blocks, scored, w_ref, stage,
    load_sem, s_pair, s_side, s1, r1, s2, r2, s3, r3, s4, r4, s_out, r_out, l_out,
):
    c = lax.axis_index("ctx")
    h = lax.axis_index("head")
    plane, side = c // 2, c % 2
    c_pair = 2 * plane + (1 - side)
    x, core = h // 2, h % 2
    h_core = 2 * x + (1 - core)
    h_x = 2 * (1 - x) + core
    h_diag = 2 * (1 - x) + (1 - core)
    own_rows = own_ref.shape[0]
    blocks = own_rows // KBLK
    part = own_rows // n_head

    load_q = pltpu.make_async_copy(q_hbm, q_ref, load_sem.at[0])
    load_w = pltpu.make_async_copy(w_hbm, w_ref, load_sem.at[1])
    load_sel = pltpu.make_async_copy(sel_hbm, sel_ref, load_sem.at[2])
    load_q.start()
    load_sel.start()
    load_w.start()

    barrier = pltpu.get_barrier_semaphore()
    for peer in (h_core, h_x, h_diag):
        pl.semaphore_signal(barrier, inc=1, device_id=(c, peer), device_id_type=MESH)

    pl.semaphore_signal(barrier, inc=1, device_id=(c_pair, h), device_id_type=MESH)

    @pl.loop(0, plane)
    def _(lower):
        pl.semaphore_signal(barrier, inc=1, device_id=(2 * lower + side, h), device_id_type=MESH)

    above = n_ctx // 2 - 1 - plane
    pl.semaphore_wait(barrier, 4 + above)

    def piece(source, quarter):
        row = quarter * part
        start = pl.multiple_of(row % KBLK, part)
        return keys.at[source * blocks + row // KBLK, pl.ds(start, part), :]

    def first_copy(source, target):
        return pltpu.make_async_remote_copy(
            src_ref=own_ref.at[pl.ds(pl.multiple_of(h * part, part), part), :],
            dst_ref=piece(source, h),
            send_sem=s1.at[target], recv_sem=r1.at[source],
            device_id=(target, h), device_id_type=MESH,
        )

    def pair_copy(source, quarter, send, recv):
        return pltpu.make_async_remote_copy(
            src_ref=own_ref.at[pl.ds(pl.multiple_of(quarter * part, part), part), :],
            dst_ref=piece(source, quarter),
            send_sem=s_pair.at[send], recv_sem=recv.at[source],
            device_id=(c_pair, h), device_id_type=MESH,
        )

    def side_copy(source):
        return pltpu.make_async_remote_copy(
            src_ref=piece(source, h), dst_ref=piece(source, h),
            send_sem=s_side.at[source], recv_sem=r1.at[source],
            device_id=(c_pair, h), device_id_type=MESH,
        )

    def relay(source, quarter, peer, send, recv):
        return pltpu.make_async_remote_copy(
            src_ref=piece(source, quarter), dst_ref=piece(source, quarter),
            send_sem=send.at[source], recv_sem=recv.at[source],
            device_id=(c, peer), device_id_type=MESH,
        )

    @pl.when(side == 0)
    def _():
        pair_copy(c, h, 0, r1).start()
        pair_copy(c, h_x, 1, r2).start()

    @pl.loop(0, above)
    def _(step):
        first_copy(c, n_ctx - 2 + side - 2 * step).start()

    for block in range(blocks):
        keys[c * blocks + block] = own_ref[block * KBLK:(block + 1) * KBLK, :]

    load_q.wait()
    per_group = heads // GROUPS
    columns = per_group * KBLK
    for pair in range(heads // 2):
        group, slot = divmod(pair, heads // (2 * GROUPS))
        lanes = slice(slot * 2 * KBLK, (slot + 1) * 2 * KBLK)
        first, second = q_ref[2 * pair], q_ref[2 * pair + 1]
        q_blocks[0, group, :, lanes] = jnp.concatenate([first[:, :KBLK], second[:, :KBLK]], axis=1)
        q_blocks[1, group, :, lanes] = jnp.concatenate([first[:, KBLK:], second[:, KBLK:]], axis=1)

    def score_source(source):
        rows = jnp.concatenate([keys[source * blocks + block] for block in range(blocks)], axis=0)
        for position in range(2):
            for group in range(GROUPS):
                result = jnp.dot(rows, q_blocks[position, group], preferred_element_type=jnp.float32)
                for block in range(blocks):
                    scored[source * blocks + block, position, group] = result[block * KBLK:(block + 1) * KBLK]

    def pass_on(source, across):
        first_copy(source, c).wait_recv()
        relay(source, h, h_core, s3, r3).start()

        if across is True:
            relay(source, h, h_x, s2, r2).start()
        else:
            @pl.when(across)
            def _():
                relay(source, h, h_x, s2, r2).start()

    def pass_second(source):
        relay(source, h_x, h_x, s2, r2).wait_recv()
        relay(source, h_x, h_core, s4, r4).start()

    def complete(source):
        relay(source, h_core, h_core, s3, r3).wait_recv()
        relay(source, h_diag, h_core, s4, r4).wait_recv()
        if dense:
            score_source(source)

    def same(step):
        return 2 * (plane - 1 - step) + side

    def other(step):
        return 2 * (plane - step) + (1 - side)

    def has_same(step):
        return (step >= 0) & (step < plane)

    def has_other(step):
        return (step >= 1 - side) & (step <= plane)

    @pl.loop(0, plane + 3)
    def _(step):
        @pl.when(has_same(step))
        def _():
            pass_on(same(step), True)
            side_copy(same(step)).start()

        @pl.when(has_other(step))
        def _():
            pass_on(other(step), step > 0)

        if dense:
            @pl.when(step == 0)
            def _():
                score_source(c)

        @pl.when(has_same(step - 1))
        def _():
            pass_second(same(step - 1))

        @pl.when(has_other(step - 1))
        def _():
            pass_second(other(step - 1))

        @pl.when(has_same(step - 2))
        def _():
            complete(same(step - 2))

        @pl.when(has_other(step - 2))
        def _():
            complete(other(step - 2))

    load_w.wait()
    load_sel.wait()

    factor = (DV + DR) ** (-0.5) * math.log2(math.e)
    key_row = lax.broadcasted_iota(jnp.int32, (SEL * KBLK, 1), 0)
    width = per_group * DV
    token = lax.broadcasted_iota(jnp.int32, (1, columns), 1) % KBLK

    def out_copy(group, target, relation):
        return pltpu.make_async_remote_copy(
            src_ref=stage.at[target, :, pl.ds(group * width, width)],
            dst_ref=out_ref.at[:, pl.ds(pl.multiple_of(h * (heads * DV) + group * width, width), width)],
            send_sem=s_out.at[relation, group], recv_sem=r_out.at[relation, group],
            device_id=(c, target), device_id_type=MESH,
        )

    def out_local(group):
        return pltpu.make_async_copy(
            stage.at[h, :, pl.ds(group * width, width)],
            out_ref.at[:, pl.ds(pl.multiple_of(h * (heads * DV) + group * width, width), width)],
            l_out.at[group],
        )

    half = KBLK // 2

    def slots_of(position):
        chosen = [sel_ref[position, slot] for slot in range(SEL)]
        return chosen, [jnp.maximum(one, 0) for one in chosen]

    def weigh(position, group):
        chosen, entry = slots_of(position)
        key_block = jnp.full((SEL * KBLK, 1), chosen[0], jnp.int32)
        for slot in range(1, SEL):
            key_block = jnp.where(key_row // KBLK == slot, chosen[slot], key_block)
        key_place = jnp.where(key_block < 0, FAR, key_block * KBLK + key_row % KBLK)
        query_place = token + (c * blocks + position) * KBLK
        if dense:
            scores = jnp.concatenate([scored[one, position, group] for one in entry], axis=0)
        else:
            rows = jnp.concatenate([keys[one] for one in entry], axis=0)
            scores = jnp.dot(rows, q_blocks[position, group], preferred_element_type=jnp.float32)
        scores = jnp.where(key_place <= query_place, scores, -1e30)
        largest = jnp.max(scores, axis=0, keepdims=True)
        powered = jnp.exp2((scores - largest) * factor)
        total = jnp.sum(powered, axis=0, keepdims=True)
        return (powered * (1.0 / total)).astype(jnp.bfloat16).T

    def finish(turn, position, group, weights):
        latent = jnp.dot(weights, kbuf[turn], preferred_element_type=jnp.float32).astype(jnp.bfloat16)
        for inner in range(per_group):
            head = group * per_group + inner
            value = jnp.dot(
                latent[inner * KBLK:(inner + 1) * KBLK], w_ref[head], preferred_element_type=jnp.float32
            ).astype(jnp.bfloat16)
            stage[2 * position, :, head * DV:(head + 1) * DV] = value[:half]
            stage[2 * position + 1, :, head * DV:(head + 1) * DV] = value[half:]

    def send(turn, group):
        if turn == 0:
            out_copy(group, h_x, 0).start()
            out_copy(group, h_diag, 1).start()
        else:
            out_copy(group, h_core, 2).start()
            out_local(group).start()

    order = [(turn, (1 - x) if turn == 0 else x, group) for turn in range(2) for group in range(GROUPS)]
    for turn in range(2):
        _, entry = slots_of((1 - x) if turn == 0 else x)
        for slot in range(SEL):
            kbuf[turn, slot * KBLK:(slot + 1) * KBLK, :] = keys[entry[slot], :, :DC]
    weights = weigh(order[0][1], order[0][2])
    for number, (turn, position, group) in enumerate(order):
        after = None
        if number + 1 < len(order):
            after = weigh(order[number + 1][1], order[number + 1][2])
        finish(turn, position, group, weights)
        send(turn, group)
        weights = after

    for group in range(GROUPS):
        out_local(group).wait()
        for relation, peer in enumerate((h_x, h_diag, h_core)):
            out_copy(group, peer, relation).wait()

    @pl.when(side == 0)
    def _():
        pair_copy(c, h, 0, r1).wait_send()
        pair_copy(c, h_x, 1, r2).wait_send()

    @pl.loop(0, above)
    def _(step):
        first_copy(c, n_ctx - 2 + side - 2 * step).wait_send()

    @pl.loop(0, c)
    def _(source):
        relay(source, h, h_core, s3, r3).wait_send()
        relay(source, h_x, h_core, s4, r4).wait_send()

    @pl.loop(0, 2 * plane)
    def _(source):
        relay(source, h, h_x, s2, r2).wait_send()

    @pl.loop(0, plane)
    def _(lower):
        side_copy(2 * lower + side).wait_send()


def per_device(queries, latent_cache, selected, value_weight):
    n_ctx, n_head = lax.axis_size("ctx"), lax.axis_size("head")
    width = DC + DR
    tokens, heads = queries.shape[:2]
    own = latent_cache.reshape(tokens, width)
    by_head = queries.transpose(1, 2, 0)
    part = tokens // n_head
    n_blocks = n_ctx * tokens // KBLK
    dense = n_blocks <= DENSE_BLOCKS
    scored_blocks = n_blocks if dense else 1
    dma = pltpu.SemaphoreType.DMA
    return pl.pallas_call(
        functools.partial(kernel, n_ctx, n_head, heads, dense),
        out_shape=jax.ShapeDtypeStruct((part, n_head * heads * DV), jnp.bfloat16),
        in_specs=[
            pl.BlockSpec(memory_space=pltpu.HBM),
            pl.BlockSpec(memory_space=pltpu.VMEM),
            pl.BlockSpec(memory_space=pl.ANY),
            pl.BlockSpec(memory_space=pl.ANY),
        ],
        out_specs=pl.BlockSpec(memory_space=pl.ANY),
        scratch_shapes=[
            pltpu.SMEM(selected.shape, jnp.int32),
            pltpu.VMEM((n_ctx * tokens // KBLK, KBLK, width), jnp.bfloat16),
            pltpu.VMEM((2, SEL * KBLK, DC), jnp.bfloat16),
            pltpu.VMEM((heads, width, tokens), jnp.bfloat16),
            pltpu.VMEM((tokens // KBLK, GROUPS, width, heads // GROUPS * KBLK), jnp.bfloat16),
            pltpu.VMEM((scored_blocks, 2, GROUPS, KBLK, heads // GROUPS * KBLK), jnp.float32),
            pltpu.VMEM((heads, DC, DV), jnp.bfloat16),
            pltpu.VMEM((n_head, part, heads * DV), jnp.bfloat16),
            dma((3,)), dma((2,)), dma((n_ctx,)),
            dma((n_ctx,)), dma((n_ctx,)),
            dma((n_ctx,)), dma((n_ctx,)),
            dma((n_ctx,)), dma((n_ctx,)),
            dma((n_ctx,)), dma((n_ctx,)),
            dma((3, GROUPS)), dma((3, GROUPS)), dma((GROUPS,)),
        ],
        compiler_params=pltpu.CompilerParams(
            collective_id=0, has_side_effects=True, vmem_limit_bytes=52 * 1024 * 1024
        ),
    )(selected, own, by_head, value_weight)


def solution(mesh):
    in_specs = (P("ctx", "head", None), P("ctx", None), P("ctx", None), P("head", None, None))
    out_specs = P(("ctx", "head"), None)
    return jax.shard_map(
        per_device, mesh=mesh, in_specs=in_specs, out_specs=out_specs, check_vma=False
    )
```

```python
import functools
import math

import jax
import jax.numpy as jnp
from jax import lax
from jax.experimental import pallas as pl
from jax.experimental.pallas import tpu as pltpu
from jax.sharding import PartitionSpec as P

DC = 512
DR = 64
DV = 128
KBLK = 64
SEL = 8
GROUPS = 4
DENSE_BLOCKS = 32
MESH = pl.DeviceIdType.MESH
FAR = 1 << 30
VMEM_LIMIT = 62 * 1024 * 1024


def kernel(
    n_ctx, n_head, heads, dense,
    sel_hbm, own_ref, q_hbm, w_hbm, out_ref,
    sel_ref, keys, kbuf, q_ref, q_blocks, scored, w_ref, stage,
    load_sem, s_pair, s_side, s1, r1, s2, r2, s3, r3, s4, r4, s_out, r_out, l_out,
):
    c = lax.axis_index("ctx")
    h = lax.axis_index("head")
    plane, side = c // 2, c % 2
    c_pair = 2 * plane + (1 - side)
    x, core = h // 2, h % 2
    h_core = 2 * x + (1 - core)
    h_x = 2 * (1 - x) + core
    h_diag = 2 * (1 - x) + (1 - core)
    own_rows = own_ref.shape[0]
    blocks = own_rows // KBLK
    part = own_rows // n_head

    load_q = pltpu.make_async_copy(q_hbm, q_ref, load_sem.at[0])
    load_w = pltpu.make_async_copy(w_hbm, w_ref, load_sem.at[1])
    load_sel = pltpu.make_async_copy(sel_hbm, sel_ref, load_sem.at[2])
    load_q.start()
    load_sel.start()
    load_w.start()

    barrier = pltpu.get_barrier_semaphore()
    for peer in (h_core, h_x, h_diag):
        pl.semaphore_signal(barrier, inc=1, device_id=(c, peer), device_id_type=MESH)

    for peer in (h, h_x):
        pl.semaphore_signal(barrier, inc=1, device_id=(c_pair, peer), device_id_type=MESH)

    @pl.loop(0, plane)
    def _(lower):
        pl.semaphore_signal(barrier, inc=1, device_id=(2 * lower + side, h), device_id_type=MESH)

    above = n_ctx // 2 - 1 - plane
    pl.semaphore_wait(barrier, 5 + above)

    def piece(source, quarter):
        row = quarter * part
        start = pl.multiple_of(row % KBLK, part)
        return keys.at[source * blocks + row // KBLK, pl.ds(start, part), :]

    def first_copy(source, target):
        return pltpu.make_async_remote_copy(
            src_ref=own_ref.at[pl.ds(pl.multiple_of(h * part, part), part), :],
            dst_ref=piece(source, h),
            send_sem=s1.at[target], recv_sem=r1.at[source],
            device_id=(target, h), device_id_type=MESH,
        )

    def pair_copy(source, quarter, send, recv):
        return pltpu.make_async_remote_copy(
            src_ref=own_ref.at[pl.ds(pl.multiple_of(quarter * part, part), part), :],
            dst_ref=piece(source, quarter),
            send_sem=s_pair.at[send], recv_sem=recv.at[source],
            device_id=(c_pair, h), device_id_type=MESH,
        )

    def side_copy(source, peer, send, recv):
        return pltpu.make_async_remote_copy(
            src_ref=piece(source, h), dst_ref=piece(source, h),
            send_sem=s_side.at[send, source], recv_sem=recv.at[source],
            device_id=(c_pair, peer), device_id_type=MESH,
        )

    def relay(source, quarter, peer, send, recv):
        return pltpu.make_async_remote_copy(
            src_ref=piece(source, quarter), dst_ref=piece(source, quarter),
            send_sem=send.at[source], recv_sem=recv.at[source],
            device_id=(c, peer), device_id_type=MESH,
        )

    @pl.when(side == 0)
    def _():
        pair_copy(c, h, 0, r1).start()
        pair_copy(c, h_x, 1, r2).start()

    @pl.loop(0, above)
    def _(step):
        first_copy(c, n_ctx - 2 + side - 2 * step).start()

    for block in range(blocks):
        keys[c * blocks + block] = own_ref[block * KBLK:(block + 1) * KBLK, :]

    load_q.wait()
    per_group = heads // GROUPS
    columns = per_group * KBLK
    for pair in range(heads // 2):
        group, slot = divmod(pair, heads // (2 * GROUPS))
        lanes = slice(slot * 2 * KBLK, (slot + 1) * 2 * KBLK)
        first, second = q_ref[2 * pair], q_ref[2 * pair + 1]
        q_blocks[0, group, :, lanes] = jnp.concatenate([first[:, :KBLK], second[:, :KBLK]], axis=1)
        q_blocks[1, group, :, lanes] = jnp.concatenate([first[:, KBLK:], second[:, KBLK:]], axis=1)

    def score_source(source):
        rows = jnp.concatenate([keys[source * blocks + block] for block in range(blocks)], axis=0)
        for position in range(2):
            for group in range(GROUPS):
                result = jnp.dot(rows, q_blocks[position, group], preferred_element_type=jnp.float32)
                for block in range(blocks):
                    scored[source * blocks + block, position, group] = result[block * KBLK:(block + 1) * KBLK]

    if dense:
        score_source(c)

    def pass_first(source):
        first_copy(source, c).wait_recv()
        relay(source, h, h_core, s3, r3).start()

    def pass_second(source):
        relay(source, h_x, h_x, s2, r2).wait_recv()
        relay(source, h_x, h_core, s4, r4).start()

    def complete(source):
        relay(source, h_core, h_core, s3, r3).wait_recv()
        relay(source, h_diag, h_core, s4, r4).wait_recv()
        if dense:
            score_source(source)

    def same(step):
        return 2 * (plane - 1 - step) + side

    def other(step):
        return 2 * (plane - step) + (1 - side)

    def has_same(step):
        return (step >= 0) & (step < plane)

    def has_other(step):
        return (step >= 1 - side) & (step <= plane)

    @pl.loop(0, plane + 3)
    def _(step):
        @pl.when(has_same(step))
        def _():
            source = same(step)
            first_copy(source, c).wait_recv()
            side_copy(source, h, 0, r1).start()
            side_copy(source, h_x, 1, r2).start()
            relay(source, h, h_x, s2, r2).start()
            relay(source, h, h_core, s3, r3).start()

        @pl.when(has_other(step - 1))
        def _():
            pass_first(other(step - 1))
            pass_second(other(step - 1))

        @pl.when(has_same(step - 2))
        def _():
            pass_second(same(step - 2))

        @pl.when(has_other(step - 2))
        def _():
            complete(other(step - 2))

        @pl.when(has_same(step - 3))
        def _():
            complete(same(step - 3))

    load_w.wait()
    load_sel.wait()

    factor = (DV + DR) ** (-0.5) * math.log2(math.e)
    key_row = lax.broadcasted_iota(jnp.int32, (SEL * KBLK, 1), 0)
    width = per_group * DV
    token = lax.broadcasted_iota(jnp.int32, (1, columns), 1) % KBLK

    def out_copy(group, target, relation):
        return pltpu.make_async_remote_copy(
            src_ref=stage.at[target, :, pl.ds(group * width, width)],
            dst_ref=out_ref.at[:, pl.ds(pl.multiple_of(h * (heads * DV) + group * width, width), width)],
            send_sem=s_out.at[relation, group], recv_sem=r_out.at[relation, group],
            device_id=(c, target), device_id_type=MESH,
        )

    def out_local(group):
        return pltpu.make_async_copy(
            stage.at[h, :, pl.ds(group * width, width)],
            out_ref.at[:, pl.ds(pl.multiple_of(h * (heads * DV) + group * width, width), width)],
            l_out.at[group],
        )

    half = KBLK // 2

    def slots_of(position):
        chosen = [sel_ref[position, slot] for slot in range(SEL)]
        return chosen, [jnp.maximum(one, 0) for one in chosen]

    def weigh(position, group):
        chosen, entry = slots_of(position)
        key_block = jnp.full((SEL * KBLK, 1), chosen[0], jnp.int32)
        for slot in range(1, SEL):
            key_block = jnp.where(key_row // KBLK == slot, chosen[slot], key_block)
        key_place = jnp.where(key_block < 0, FAR, key_block * KBLK + key_row % KBLK)
        query_place = token + (c * blocks + position) * KBLK
        if dense:
            scores = jnp.concatenate([scored[one, position, group] for one in entry], axis=0)
        else:
            rows = jnp.concatenate([keys[one] for one in entry], axis=0)
            scores = jnp.dot(rows, q_blocks[position, group], preferred_element_type=jnp.float32)
        scores = jnp.where(key_place <= query_place, scores, -1e30)
        largest = jnp.max(scores, axis=0, keepdims=True)
        powered = jnp.exp2((scores - largest) * factor)
        total = jnp.sum(powered, axis=0, keepdims=True)
        return (powered * (1.0 / total)).astype(jnp.bfloat16).T

    def finish(turn, position, group, weights):
        latent = jnp.dot(weights, kbuf[turn], preferred_element_type=jnp.float32).astype(jnp.bfloat16)
        for inner in range(per_group):
            head = group * per_group + inner
            value = jnp.dot(
                latent[inner * KBLK:(inner + 1) * KBLK], w_ref[head], preferred_element_type=jnp.float32
            ).astype(jnp.bfloat16)
            stage[2 * position, :, head * DV:(head + 1) * DV] = value[:half]
            stage[2 * position + 1, :, head * DV:(head + 1) * DV] = value[half:]

    def send(turn, group):
        if turn == 0:
            out_copy(group, h_x, 0).start()
            out_copy(group, h_diag, 1).start()
        else:
            out_copy(group, h_core, 2).start()
            out_local(group).start()

    order = [(turn, (1 - x) if turn == 0 else x, group) for turn in range(2) for group in range(GROUPS)]
    for turn in range(2):
        _, entry = slots_of((1 - x) if turn == 0 else x)
        for slot in range(SEL):
            kbuf[turn, slot * KBLK:(slot + 1) * KBLK, :] = keys[entry[slot], :, :DC]
    weights = weigh(order[0][1], order[0][2])
    for number, (turn, position, group) in enumerate(order):
        after = None
        if number + 1 < len(order):
            after = weigh(order[number + 1][1], order[number + 1][2])
        finish(turn, position, group, weights)
        send(turn, group)
        weights = after

    for group in range(GROUPS):
        out_local(group).wait()
        for relation, peer in enumerate((h_x, h_diag, h_core)):
            out_copy(group, peer, relation).wait()

    @pl.when(side == 0)
    def _():
        pair_copy(c, h, 0, r1).wait_send()
        pair_copy(c, h_x, 1, r2).wait_send()

    @pl.loop(0, above)
    def _(step):
        first_copy(c, n_ctx - 2 + side - 2 * step).wait_send()

    @pl.loop(0, c)
    def _(source):
        relay(source, h, h_core, s3, r3).wait_send()
        relay(source, h_x, h_core, s4, r4).wait_send()

    @pl.loop(0, plane)
    def _(lower):
        source = 2 * lower + side
        relay(source, h, h_x, s2, r2).wait_send()
        side_copy(source, h, 0, r1).wait_send()
        side_copy(source, h_x, 1, r2).wait_send()


def per_device(queries, latent_cache, selected, value_weight):
    n_ctx, n_head = lax.axis_size("ctx"), lax.axis_size("head")
    width = DC + DR
    tokens, heads = queries.shape[:2]
    own = latent_cache.reshape(tokens, width)
    by_head = queries.transpose(1, 2, 0)
    part = tokens // n_head
    n_blocks = n_ctx * tokens // KBLK
    dense = n_blocks <= DENSE_BLOCKS
    scored_blocks = n_blocks if dense else 1
    dma = pltpu.SemaphoreType.DMA
    return pl.pallas_call(
        functools.partial(kernel, n_ctx, n_head, heads, dense),
        out_shape=jax.ShapeDtypeStruct((part, n_head * heads * DV), jnp.bfloat16),
        in_specs=[
            pl.BlockSpec(memory_space=pltpu.HBM),
            pl.BlockSpec(memory_space=pltpu.VMEM),
            pl.BlockSpec(memory_space=pl.ANY),
            pl.BlockSpec(memory_space=pl.ANY),
        ],
        out_specs=pl.BlockSpec(memory_space=pl.ANY),
        scratch_shapes=[
            pltpu.SMEM(selected.shape, jnp.int32),
            pltpu.VMEM((n_ctx * tokens // KBLK, KBLK, width), jnp.bfloat16),
            pltpu.VMEM((2, SEL * KBLK, DC), jnp.bfloat16),
            pltpu.VMEM((heads, width, tokens), jnp.bfloat16),
            pltpu.VMEM((tokens // KBLK, GROUPS, width, heads // GROUPS * KBLK), jnp.bfloat16),
            pltpu.VMEM((scored_blocks, 2, GROUPS, KBLK, heads // GROUPS * KBLK), jnp.float32),
            pltpu.VMEM((heads, DC, DV), jnp.bfloat16),
            pltpu.VMEM((n_head, part, heads * DV), jnp.bfloat16),
            dma((3,)), dma((2,)), dma((2, n_ctx)),
            dma((n_ctx,)), dma((n_ctx,)),
            dma((n_ctx,)), dma((n_ctx,)),
            dma((n_ctx,)), dma((n_ctx,)),
            dma((n_ctx,)), dma((n_ctx,)),
            dma((3, GROUPS)), dma((3, GROUPS)), dma((GROUPS,)),
        ],
        compiler_params=pltpu.CompilerParams(
            collective_id=0, has_side_effects=True, vmem_limit_bytes=VMEM_LIMIT
        ),
    )(selected, own, by_head, value_weight)


def solution(mesh):
    in_specs = (P("ctx", "head", None), P("ctx", None), P("ctx", None), P("head", None, None))
    out_specs = P(("ctx", "head"), None)
    return jax.shard_map(
        per_device, mesh=mesh, in_specs=in_specs, out_specs=out_specs, check_vma=False
    )
```

```python
import functools
import math

import jax
import jax.numpy as jnp
from jax import lax
from jax.experimental import pallas as pl
from jax.experimental.pallas import tpu as pltpu
from jax.sharding import PartitionSpec as P

DC = 512
DR = 64
DV = 128
KBLK = 64
SEL = 8
GROUPS = 4
MESH = pl.DeviceIdType.MESH
FAR = 1 << 30
VMEM_LIMIT = 52 * 1024 * 1024


def kernel(
    n_ctx, n_head, heads,
    sel_hbm, own_ref, q_hbm, w_hbm, out_ref,
    sel_ref, keys, kbuf, q_ref, q_blocks, w_ref, stage,
    load_sem, s_pair, s_side, s1, r1, s2, r2, s3, r3, s4, r4, s_out, r_out, l_out,
):
    c = lax.axis_index("ctx")
    h = lax.axis_index("head")
    plane, side = c // 2, c % 2
    c_pair = 2 * plane + (1 - side)
    x, core = h // 2, h % 2
    h_core = 2 * x + (1 - core)
    h_x = 2 * (1 - x) + core
    h_diag = 2 * (1 - x) + (1 - core)
    own_rows = own_ref.shape[0]
    blocks = own_rows // KBLK
    part = own_rows // n_head

    load_q = pltpu.make_async_copy(q_hbm, q_ref, load_sem.at[0])
    load_w = pltpu.make_async_copy(w_hbm, w_ref, load_sem.at[1])
    load_sel = pltpu.make_async_copy(sel_hbm, sel_ref, load_sem.at[2])
    load_q.start()
    load_sel.start()
    load_w.start()

    barrier = pltpu.get_barrier_semaphore()
    for peer in (h_core, h_x, h_diag):
        pl.semaphore_signal(barrier, inc=1, device_id=(c, peer), device_id_type=MESH)

    for peer in (h, h_x):
        pl.semaphore_signal(barrier, inc=1, device_id=(c_pair, peer), device_id_type=MESH)

    @pl.loop(0, plane)
    def _(lower):
        pl.semaphore_signal(barrier, inc=1, device_id=(2 * lower + side, h), device_id_type=MESH)

    above = n_ctx // 2 - 1 - plane
    pl.semaphore_wait(barrier, 5 + above)

    def piece(source, quarter):
        row = quarter * part
        start = pl.multiple_of(row % KBLK, part)
        return keys.at[source * blocks + row // KBLK, pl.ds(start, part), :]

    def first_copy(source, target):
        return pltpu.make_async_remote_copy(
            src_ref=own_ref.at[pl.ds(pl.multiple_of(h * part, part), part), :],
            dst_ref=piece(source, h),
            send_sem=s1.at[target], recv_sem=r1.at[source],
            device_id=(target, h), device_id_type=MESH,
        )

    def pair_copy(source, quarter, send, recv):
        return pltpu.make_async_remote_copy(
            src_ref=own_ref.at[pl.ds(pl.multiple_of(quarter * part, part), part), :],
            dst_ref=piece(source, quarter),
            send_sem=s_pair.at[send], recv_sem=recv.at[source],
            device_id=(c_pair, h), device_id_type=MESH,
        )

    def side_copy(source, peer, send, recv):
        return pltpu.make_async_remote_copy(
            src_ref=piece(source, h), dst_ref=piece(source, h),
            send_sem=s_side.at[send, source], recv_sem=recv.at[source],
            device_id=(c_pair, peer), device_id_type=MESH,
        )

    def relay(source, quarter, peer, send, recv):
        return pltpu.make_async_remote_copy(
            src_ref=piece(source, quarter), dst_ref=piece(source, quarter),
            send_sem=send.at[source], recv_sem=recv.at[source],
            device_id=(c, peer), device_id_type=MESH,
        )

    @pl.when(side == 0)
    def _():
        pair_copy(c, h, 0, r1).start()
        pair_copy(c, h_x, 1, r2).start()

    @pl.loop(0, above)
    def _(step):
        first_copy(c, n_ctx - 2 + side - 2 * step).start()

    for block in range(blocks):
        keys[c * blocks + block] = own_ref[block * KBLK:(block + 1) * KBLK, :]

    load_q.wait()
    per_group = heads // GROUPS
    columns = per_group * KBLK
    for pair in range(heads // 2):
        group, slot = divmod(pair, heads // (2 * GROUPS))
        lanes = slice(slot * 2 * KBLK, (slot + 1) * 2 * KBLK)
        first, second = q_ref[2 * pair], q_ref[2 * pair + 1]
        q_blocks[0, group, :, lanes] = jnp.concatenate([first[:, :KBLK], second[:, :KBLK]], axis=1)
        q_blocks[1, group, :, lanes] = jnp.concatenate([first[:, KBLK:], second[:, KBLK:]], axis=1)

    def pass_first(source):
        first_copy(source, c).wait_recv()
        relay(source, h, h_core, s3, r3).start()

    def pass_second(source):
        relay(source, h_x, h_x, s2, r2).wait_recv()
        relay(source, h_x, h_core, s4, r4).start()

    def complete(source):
        relay(source, h_core, h_core, s3, r3).wait_recv()
        relay(source, h_diag, h_core, s4, r4).wait_recv()

    def same(step):
        return 2 * (plane - 1 - step) + side

    def other(step):
        return 2 * (plane - step) + (1 - side)

    def has_same(step):
        return (step >= 0) & (step < plane)

    def has_other(step):
        return (step >= 1 - side) & (step <= plane)

    @pl.loop(0, plane + 3)
    def _(step):
        @pl.when(has_same(step))
        def _():
            source = same(step)
            first_copy(source, c).wait_recv()
            side_copy(source, h, 0, r1).start()
            side_copy(source, h_x, 1, r2).start()
            relay(source, h, h_x, s2, r2).start()
            relay(source, h, h_core, s3, r3).start()

        @pl.when(has_other(step - 1))
        def _():
            pass_first(other(step - 1))
            pass_second(other(step - 1))

        @pl.when(has_same(step - 2))
        def _():
            pass_second(same(step - 2))

        @pl.when(has_other(step - 2))
        def _():
            complete(other(step - 2))

        @pl.when(has_same(step - 3))
        def _():
            complete(same(step - 3))

    load_w.wait()
    load_sel.wait()

    factor = (DV + DR) ** (-0.5) * math.log2(math.e)
    key_row = lax.broadcasted_iota(jnp.int32, (SEL * KBLK, 1), 0)
    width = per_group * DV
    token = lax.broadcasted_iota(jnp.int32, (1, columns), 1) % KBLK

    def out_copy(group, target, relation):
        return pltpu.make_async_remote_copy(
            src_ref=stage.at[target, :, pl.ds(group * width, width)],
            dst_ref=out_ref.at[:, pl.ds(pl.multiple_of(h * (heads * DV) + group * width, width), width)],
            send_sem=s_out.at[relation, group], recv_sem=r_out.at[relation, group],
            device_id=(c, target), device_id_type=MESH,
        )

    def out_local(group):
        return pltpu.make_async_copy(
            stage.at[h, :, pl.ds(group * width, width)],
            out_ref.at[:, pl.ds(pl.multiple_of(h * (heads * DV) + group * width, width), width)],
            l_out.at[group],
        )

    half = KBLK // 2

    def slots_of(position):
        chosen = [sel_ref[position, slot] for slot in range(SEL)]
        return chosen, [jnp.maximum(one, 0) for one in chosen]

    def weigh(turn, position, group):
        chosen, _ = slots_of(position)
        key_block = jnp.full((SEL * KBLK, 1), chosen[0], jnp.int32)
        for slot in range(1, SEL):
            key_block = jnp.where(key_row // KBLK == slot, chosen[slot], key_block)
        key_place = jnp.where(key_block < 0, FAR, key_block * KBLK + key_row % KBLK)
        query_place = token + (c * blocks + position) * KBLK
        scores = jnp.dot(kbuf[turn], q_blocks[position, group], preferred_element_type=jnp.float32)
        scores = jnp.where(key_place <= query_place, scores, -1e30)
        largest = jnp.max(scores, axis=0, keepdims=True)
        powered = jnp.exp2((scores - largest) * factor)
        total = jnp.sum(powered, axis=0, keepdims=True)
        return (powered * (1.0 / total)).astype(jnp.bfloat16).T

    def finish(turn, position, group, weights):
        latent = jnp.dot(weights, kbuf[turn, :, :DC], preferred_element_type=jnp.float32).astype(jnp.bfloat16)
        for inner in range(per_group):
            head = group * per_group + inner
            value = jnp.dot(
                latent[inner * KBLK:(inner + 1) * KBLK], w_ref[head], preferred_element_type=jnp.float32
            ).astype(jnp.bfloat16)
            stage[2 * position, :, head * DV:(head + 1) * DV] = value[:half]
            stage[2 * position + 1, :, head * DV:(head + 1) * DV] = value[half:]

    def send(turn, group):
        if turn == 0:
            out_copy(group, h_x, 0).start()
            out_copy(group, h_diag, 1).start()
        else:
            out_copy(group, h_core, 2).start()
            out_local(group).start()

    order = [(turn, (1 - x) if turn == 0 else x, group) for turn in range(2) for group in range(GROUPS)]
    for turn in range(2):
        _, entry = slots_of((1 - x) if turn == 0 else x)
        for slot in range(SEL):
            kbuf[turn, slot * KBLK:(slot + 1) * KBLK, :] = keys[entry[slot]]
    weights = weigh(*order[0])
    for number, (turn, position, group) in enumerate(order):
        after = None
        if number + 1 < len(order):
            after = weigh(*order[number + 1])
        finish(turn, position, group, weights)
        send(turn, group)
        weights = after

    for group in range(GROUPS):
        out_local(group).wait()
        for relation, peer in enumerate((h_x, h_diag, h_core)):
            out_copy(group, peer, relation).wait()

    @pl.when(side == 0)
    def _():
        pair_copy(c, h, 0, r1).wait_send()
        pair_copy(c, h_x, 1, r2).wait_send()

    @pl.loop(0, above)
    def _(step):
        first_copy(c, n_ctx - 2 + side - 2 * step).wait_send()

    @pl.loop(0, c)
    def _(source):
        relay(source, h, h_core, s3, r3).wait_send()
        relay(source, h_x, h_core, s4, r4).wait_send()

    @pl.loop(0, plane)
    def _(lower):
        source = 2 * lower + side
        relay(source, h, h_x, s2, r2).wait_send()
        side_copy(source, h, 0, r1).wait_send()
        side_copy(source, h_x, 1, r2).wait_send()


def per_device(queries, latent_cache, selected, value_weight):
    n_ctx, n_head = lax.axis_size("ctx"), lax.axis_size("head")
    width = DC + DR
    tokens, heads = queries.shape[:2]
    own = latent_cache.reshape(tokens, width)
    by_head = queries.transpose(1, 2, 0)
    part = tokens // n_head
    dma = pltpu.SemaphoreType.DMA
    return pl.pallas_call(
        functools.partial(kernel, n_ctx, n_head, heads),
        out_shape=jax.ShapeDtypeStruct((part, n_head * heads * DV), jnp.bfloat16),
        in_specs=[
            pl.BlockSpec(memory_space=pltpu.HBM),
            pl.BlockSpec(memory_space=pltpu.VMEM),
            pl.BlockSpec(memory_space=pl.ANY),
            pl.BlockSpec(memory_space=pl.ANY),
        ],
        out_specs=pl.BlockSpec(memory_space=pl.ANY),
        scratch_shapes=[
            pltpu.SMEM(selected.shape, jnp.int32),
            pltpu.VMEM((n_ctx * tokens // KBLK, KBLK, width), jnp.bfloat16),
            pltpu.VMEM((2, SEL * KBLK, width), jnp.bfloat16),
            pltpu.VMEM((heads, width, tokens), jnp.bfloat16),
            pltpu.VMEM((tokens // KBLK, GROUPS, width, heads // GROUPS * KBLK), jnp.bfloat16),
            pltpu.VMEM((heads, DC, DV), jnp.bfloat16),
            pltpu.VMEM((n_head, part, heads * DV), jnp.bfloat16),
            dma((3,)), dma((2,)), dma((2, n_ctx)),
            dma((n_ctx,)), dma((n_ctx,)),
            dma((n_ctx,)), dma((n_ctx,)),
            dma((n_ctx,)), dma((n_ctx,)),
            dma((n_ctx,)), dma((n_ctx,)),
            dma((3, GROUPS)), dma((3, GROUPS)), dma((GROUPS,)),
        ],
        compiler_params=pltpu.CompilerParams(
            collective_id=0, has_side_effects=True, vmem_limit_bytes=VMEM_LIMIT
        ),
    )(selected, own, by_head, value_weight)


def solution(mesh):
    in_specs = (P("ctx", "head", None), P("ctx", None), P("ctx", None), P("head", None, None))
    out_specs = P(("ctx", "head"), None)
    return jax.shard_map(
        per_device, mesh=mesh, in_specs=in_specs, out_specs=out_specs, check_vma=False
    )
```

```python
import functools
import math

import jax
import jax.numpy as jnp
from jax import lax
from jax.experimental import pallas as pl
from jax.experimental.pallas import tpu as pltpu
from jax.sharding import PartitionSpec as P

DC = 512
DR = 64
DV = 128
KBLK = 64
SEL = 8
GROUPS = 4
STORES = 4
MESH = pl.DeviceIdType.MESH
FAR = 1 << 30
VMEM_LIMIT = 52 * 1024 * 1024


def kernel(
    n_ctx, n_head, heads,
    sel_hbm, own_ref, q_hbm, w_hbm, out_ref,
    sel_ref, keys, kbuf, q_ref, q_blocks, w_ref, stage,
    load_sem, s_pair, s_side, s1, r1, s2, r2, s3, r3, s4, r4, s_out, r_out, l_out,
):
    c = lax.axis_index("ctx")
    h = lax.axis_index("head")
    plane, side = c // 2, c % 2
    c_pair = 2 * plane + (1 - side)
    x, core = h // 2, h % 2
    h_core = 2 * x + (1 - core)
    h_x = 2 * (1 - x) + core
    h_diag = 2 * (1 - x) + (1 - core)
    own_rows = own_ref.shape[0]
    blocks = own_rows // KBLK
    part = own_rows // n_head

    load_q = pltpu.make_async_copy(q_hbm, q_ref, load_sem.at[0])
    load_w = pltpu.make_async_copy(w_hbm, w_ref, load_sem.at[1])
    load_sel = pltpu.make_async_copy(sel_hbm, sel_ref, load_sem.at[2])
    load_q.start()
    load_sel.start()
    load_w.start()

    barrier = pltpu.get_barrier_semaphore()
    for peer in (h_core, h_x, h_diag):
        pl.semaphore_signal(barrier, inc=1, device_id=(c, peer), device_id_type=MESH)

    for peer in (h, h_x):
        pl.semaphore_signal(barrier, inc=1, device_id=(c_pair, peer), device_id_type=MESH)

    @pl.loop(0, plane)
    def _(lower):
        pl.semaphore_signal(barrier, inc=1, device_id=(2 * lower + side, h), device_id_type=MESH)

    above = n_ctx // 2 - 1 - plane
    pl.semaphore_wait(barrier, 5 + above)

    def piece(source, quarter):
        row = quarter * part
        start = pl.multiple_of(row % KBLK, part)
        return keys.at[source * blocks + row // KBLK, pl.ds(start, part), :]

    def first_copy(source, target):
        return pltpu.make_async_remote_copy(
            src_ref=own_ref.at[pl.ds(pl.multiple_of(h * part, part), part), :],
            dst_ref=piece(source, h),
            send_sem=s1.at[target], recv_sem=r1.at[source],
            device_id=(target, h), device_id_type=MESH,
        )

    def pair_copy(source, quarter, send, recv):
        return pltpu.make_async_remote_copy(
            src_ref=own_ref.at[pl.ds(pl.multiple_of(quarter * part, part), part), :],
            dst_ref=piece(source, quarter),
            send_sem=s_pair.at[send], recv_sem=recv.at[source],
            device_id=(c_pair, h), device_id_type=MESH,
        )

    def side_copy(source, peer, send, recv):
        return pltpu.make_async_remote_copy(
            src_ref=piece(source, h), dst_ref=piece(source, h),
            send_sem=s_side.at[send, source], recv_sem=recv.at[source],
            device_id=(c_pair, peer), device_id_type=MESH,
        )

    def relay(source, quarter, peer, send, recv):
        return pltpu.make_async_remote_copy(
            src_ref=piece(source, quarter), dst_ref=piece(source, quarter),
            send_sem=send.at[source], recv_sem=recv.at[source],
            device_id=(c, peer), device_id_type=MESH,
        )

    @pl.when(side == 0)
    def _():
        pair_copy(c, h, 0, r1).start()
        pair_copy(c, h_x, 1, r2).start()

    @pl.loop(0, above)
    def _(step):
        first_copy(c, n_ctx - 2 + side - 2 * step).start()

    for block in range(blocks):
        keys[c * blocks + block] = own_ref[block * KBLK:(block + 1) * KBLK, :]

    load_q.wait()
    per_group = heads // GROUPS
    columns = per_group * KBLK
    for pair in range(heads // 2):
        group, slot = divmod(pair, heads // (2 * GROUPS))
        lanes = slice(slot * 2 * KBLK, (slot + 1) * 2 * KBLK)
        first, second = q_ref[2 * pair], q_ref[2 * pair + 1]
        q_blocks[0, group, :, lanes] = jnp.concatenate([first[:, :KBLK], second[:, :KBLK]], axis=1)
        q_blocks[1, group, :, lanes] = jnp.concatenate([first[:, KBLK:], second[:, KBLK:]], axis=1)

    def pass_first(source):
        first_copy(source, c).wait_recv()
        relay(source, h, h_core, s3, r3).start()

    def pass_second(source):
        relay(source, h_x, h_x, s2, r2).wait_recv()
        relay(source, h_x, h_core, s4, r4).start()

    def complete(source):
        relay(source, h_core, h_core, s3, r3).wait_recv()
        relay(source, h_diag, h_core, s4, r4).wait_recv()

    def same(step):
        return 2 * (plane - 1 - step) + side

    def other(step):
        return 2 * (plane - step) + (1 - side)

    def has_same(step):
        return (step >= 0) & (step < plane)

    def has_other(step):
        return (step >= 1 - side) & (step <= plane)

    @pl.loop(0, plane + 3)
    def _(step):
        @pl.when(has_same(step))
        def _():
            source = same(step)
            first_copy(source, c).wait_recv()
            side_copy(source, h, 0, r1).start()
            side_copy(source, h_x, 1, r2).start()
            relay(source, h, h_x, s2, r2).start()
            relay(source, h, h_core, s3, r3).start()

        @pl.when(has_other(step - 1))
        def _():
            pass_first(other(step - 1))
            pass_second(other(step - 1))

        @pl.when(has_same(step - 2))
        def _():
            pass_second(same(step - 2))

        @pl.when(has_other(step - 2))
        def _():
            complete(other(step - 2))

        @pl.when(has_same(step - 3))
        def _():
            complete(same(step - 3))

    load_w.wait()
    load_sel.wait()

    factor = (DV + DR) ** (-0.5) * math.log2(math.e)
    key_row = lax.broadcasted_iota(jnp.int32, (SEL * KBLK, 1), 0)
    width = per_group * DV
    token = lax.broadcasted_iota(jnp.int32, (1, columns), 1) % KBLK

    def out_copy(group, target, relation):
        return pltpu.make_async_remote_copy(
            src_ref=stage.at[target, :, pl.ds(group * width, width)],
            dst_ref=out_ref.at[:, pl.ds(pl.multiple_of(h * (heads * DV) + group * width, width), width)],
            send_sem=s_out.at[relation, group], recv_sem=r_out.at[relation, group],
            device_id=(c, target), device_id_type=MESH,
        )

    def out_local(group):
        return pltpu.make_async_copy(
            stage.at[h, :, pl.ds(group * width, width)],
            out_ref.at[:, pl.ds(pl.multiple_of(h * (heads * DV) + group * width, width), width)],
            l_out.at[group],
        )

    half = KBLK // 2

    def slots_of(position):
        chosen = [sel_ref[position, slot] for slot in range(SEL)]
        return chosen, [jnp.maximum(one, 0) for one in chosen]

    def weigh(turn, position, group):
        chosen, _ = slots_of(position)
        key_block = jnp.full((SEL * KBLK, 1), chosen[0], jnp.int32)
        for slot in range(1, SEL):
            key_block = jnp.where(key_row // KBLK == slot, chosen[slot], key_block)
        key_place = jnp.where(key_block < 0, FAR, key_block * KBLK + key_row % KBLK)
        query_place = token + (c * blocks + position) * KBLK
        scores = jnp.dot(kbuf[turn], q_blocks[position, group], preferred_element_type=jnp.float32)
        scores = jnp.where(key_place <= query_place, scores, -1e30)
        largest = jnp.max(scores, axis=0, keepdims=True)
        powered = jnp.exp2((scores - largest) * factor)
        total = jnp.sum(powered, axis=0, keepdims=True)
        return (powered * (1.0 / total)).astype(jnp.bfloat16).T

    def finish(turn, position, group, weights):
        latent = jnp.dot(weights, kbuf[turn, :, :DC], preferred_element_type=jnp.float32).astype(jnp.bfloat16)
        for inner in range(per_group):
            head = group * per_group + inner
            value = jnp.dot(
                latent[inner * KBLK:(inner + 1) * KBLK], w_ref[head], preferred_element_type=jnp.float32
            ).astype(jnp.bfloat16)
            stage[2 * position, :, head * DV:(head + 1) * DV] = value[:half]
            stage[2 * position + 1, :, head * DV:(head + 1) * DV] = value[half:]

    def send(turn, group):
        if turn == 0:
            out_copy(group, h_x, 0).start()
            out_copy(group, h_diag, 1).start()
        else:
            out_copy(group, h_core, 2).start()
            out_local(group).start()

    order = [(turn, (1 - x) if turn == 0 else x, group) for turn in range(2) for group in range(GROUPS)]

    def assemble(turn, position):
        _, entry = slots_of(position)
        for slot in range(SEL):
            kbuf[turn, slot * KBLK:(slot + 1) * KBLK, :] = keys[entry[slot]]

    assemble(0, 1 - x)
    weights = weigh(*order[0])
    for number, (turn, position, group) in enumerate(order):
        after = None
        if number == 0:
            assemble(1, x)
        if number + 1 < len(order):
            after = weigh(*order[number + 1])
        finish(turn, position, group, weights)
        send(turn, group)
        weights = after

    for group in range(GROUPS):
        out_local(group).wait()
        for relation, peer in enumerate((h_x, h_diag, h_core)):
            out_copy(group, peer, relation).wait()

    @pl.when(side == 0)
    def _():
        pair_copy(c, h, 0, r1).wait_send()
        pair_copy(c, h_x, 1, r2).wait_send()

    @pl.loop(0, above)
    def _(step):
        first_copy(c, n_ctx - 2 + side - 2 * step).wait_send()

    @pl.loop(0, c)
    def _(source):
        relay(source, h, h_core, s3, r3).wait_send()
        relay(source, h_x, h_core, s4, r4).wait_send()

    @pl.loop(0, plane)
    def _(lower):
        source = 2 * lower + side
        relay(source, h, h_x, s2, r2).wait_send()
        side_copy(source, h, 0, r1).wait_send()
        side_copy(source, h_x, 1, r2).wait_send()


def store(landed, out_ref, sems):
    span = landed.shape[1] // STORES
    copies = [
        pltpu.make_async_copy(
            landed.at[:, pl.ds(index * span, span)], out_ref.at[:, pl.ds(index * span, span)], sems.at[index]
        )
        for index in range(STORES)
    ]
    for copy in copies:
        copy.start()
    for copy in copies:
        copy.wait()


def per_device(queries, latent_cache, selected, value_weight):
    n_ctx, n_head = lax.axis_size("ctx"), lax.axis_size("head")
    width = DC + DR
    tokens, heads = queries.shape[:2]
    own = latent_cache.reshape(tokens, width)
    by_head = queries.transpose(1, 2, 0)
    part = tokens // n_head
    dma = pltpu.SemaphoreType.DMA
    chosen = jnp.maximum(selected, -1)
    landed = pl.pallas_call(
        functools.partial(kernel, n_ctx, n_head, heads),
        out_shape=jax.ShapeDtypeStruct((part, n_head * heads * DV), jnp.bfloat16),
        in_specs=[
            pl.BlockSpec(memory_space=pltpu.HBM),
            pl.BlockSpec(memory_space=pltpu.VMEM),
            pl.BlockSpec(memory_space=pl.ANY),
            pl.BlockSpec(memory_space=pl.ANY),
        ],
        out_specs=pl.BlockSpec(memory_space=pl.ANY),
        scratch_shapes=[
            pltpu.SMEM(selected.shape, jnp.int32),
            pltpu.VMEM((n_ctx * tokens // KBLK, KBLK, width), jnp.bfloat16),
            pltpu.VMEM((2, SEL * KBLK, width), jnp.bfloat16),
            pltpu.VMEM((heads, width, tokens), jnp.bfloat16),
            pltpu.VMEM((tokens // KBLK, GROUPS, width, heads // GROUPS * KBLK), jnp.bfloat16),
            pltpu.VMEM((heads, DC, DV), jnp.bfloat16),
            pltpu.VMEM((n_head, part, heads * DV), jnp.bfloat16),
            dma((3,)), dma((2,)), dma((2, n_ctx)),
            dma((n_ctx,)), dma((n_ctx,)),
            dma((n_ctx,)), dma((n_ctx,)),
            dma((n_ctx,)), dma((n_ctx,)),
            dma((n_ctx,)), dma((n_ctx,)),
            dma((3, GROUPS)), dma((3, GROUPS)), dma((GROUPS,)),
        ],
        compiler_params=pltpu.CompilerParams(
            collective_id=0, has_side_effects=True, vmem_limit_bytes=VMEM_LIMIT
        ),
    )(chosen, own, by_head, value_weight)
    return pl.pallas_call(
        store,
        out_shape=jax.ShapeDtypeStruct(landed.shape, landed.dtype),
        in_specs=[pl.BlockSpec(memory_space=pl.ANY)],
        out_specs=pl.BlockSpec(memory_space=pl.ANY),
        scratch_shapes=[dma((STORES,))],
    )(landed)


def solution(mesh):
    in_specs = (P("ctx", "head", None), P("ctx", None), P("ctx", None), P("head", None, None))
    out_specs = P(("ctx", "head"), None)
    return jax.shard_map(
        per_device, mesh=mesh, in_specs=in_specs, out_specs=out_specs, check_vma=False
    )
```

```python
import functools
import math

import jax
import jax.numpy as jnp
from jax import lax
from jax.experimental import pallas as pl
from jax.experimental.pallas import tpu as pltpu
from jax.sharding import PartitionSpec as P

DC = 512
DR = 64
DV = 128
KBLK = 64
SEL = 8
GROUPS = 4
MESH = pl.DeviceIdType.MESH
FAR = 1 << 30
VMEM_LIMIT = 52 * 1024 * 1024


def kernel(
    n_ctx, n_head, heads,
    sel_hbm, own_ref, q_hbm, w_hbm, out_ref,
    sel_ref, keys, kbuf, q_ref, q_blocks, w_ref, stage,
    load_sem, s_pair, s_side, s1, r1, s2, r2, s3, r3, s4, r4, s_out, r_out, l_out,
):
    c = lax.axis_index("ctx")
    h = lax.axis_index("head")
    plane, side = c // 2, c % 2
    c_pair = 2 * plane + (1 - side)
    x, core = h // 2, h % 2
    h_core = 2 * x + (1 - core)
    h_x = 2 * (1 - x) + core
    h_diag = 2 * (1 - x) + (1 - core)
    own_rows = own_ref.shape[0]
    blocks = own_rows // KBLK
    part = own_rows // n_head

    load_q = pltpu.make_async_copy(q_hbm, q_ref, load_sem.at[0])
    load_w = pltpu.make_async_copy(w_hbm, w_ref, load_sem.at[1])
    load_sel = pltpu.make_async_copy(sel_hbm, sel_ref, load_sem.at[2])
    load_q.start()
    load_sel.start()
    load_w.start()

    barrier = pltpu.get_barrier_semaphore()
    for peer in (h_core, h_x, h_diag):
        pl.semaphore_signal(barrier, inc=1, device_id=(c, peer), device_id_type=MESH)

    for peer in (h, h_x):
        pl.semaphore_signal(barrier, inc=1, device_id=(c_pair, peer), device_id_type=MESH)

    @pl.loop(0, plane)
    def _(lower):
        pl.semaphore_signal(barrier, inc=1, device_id=(2 * lower + side, h), device_id_type=MESH)

    above = n_ctx // 2 - 1 - plane
    pl.semaphore_wait(barrier, 5 + above)

    def piece(source, quarter):
        row = quarter * part
        start = pl.multiple_of(row % KBLK, part)
        return keys.at[source * blocks + row // KBLK, pl.ds(start, part), :]

    def first_copy(source, target):
        return pltpu.make_async_remote_copy(
            src_ref=own_ref.at[pl.ds(pl.multiple_of(h * part, part), part), :],
            dst_ref=piece(source, h),
            send_sem=s1.at[target], recv_sem=r1.at[source],
            device_id=(target, h), device_id_type=MESH,
        )

    def pair_copy(source, quarter, send, recv):
        return pltpu.make_async_remote_copy(
            src_ref=own_ref.at[pl.ds(pl.multiple_of(quarter * part, part), part), :],
            dst_ref=piece(source, quarter),
            send_sem=s_pair.at[send], recv_sem=recv.at[source],
            device_id=(c_pair, h), device_id_type=MESH,
        )

    def side_copy(source, peer, send, recv):
        return pltpu.make_async_remote_copy(
            src_ref=piece(source, h), dst_ref=piece(source, h),
            send_sem=s_side.at[send, source], recv_sem=recv.at[source],
            device_id=(c_pair, peer), device_id_type=MESH,
        )

    def relay(source, quarter, peer, send, recv):
        return pltpu.make_async_remote_copy(
            src_ref=piece(source, quarter), dst_ref=piece(source, quarter),
            send_sem=send.at[source], recv_sem=recv.at[source],
            device_id=(c, peer), device_id_type=MESH,
        )

    @pl.loop(0, above)
    def _(step):
        first_copy(c, n_ctx - 2 + side - 2 * step).start()

    @pl.when(side == 0)
    def _():
        pair_copy(c, h, 0, r1).start()
        pair_copy(c, h_x, 1, r2).start()

    for block in range(blocks):
        keys[c * blocks + block] = own_ref[block * KBLK:(block + 1) * KBLK, :]

    per_group = heads // GROUPS
    columns = per_group * KBLK

    def build_queries():
        load_q.wait()
        for pair in range(heads // 2):
            group, slot = divmod(pair, heads // (2 * GROUPS))
            lanes = slice(slot * 2 * KBLK, (slot + 1) * 2 * KBLK)
            first, second = q_ref[2 * pair], q_ref[2 * pair + 1]
            q_blocks[0, group, :, lanes] = jnp.concatenate([first[:, :KBLK], second[:, :KBLK]], axis=1)
            q_blocks[1, group, :, lanes] = jnp.concatenate([first[:, KBLK:], second[:, KBLK:]], axis=1)

    def pass_first(source):
        first_copy(source, c).wait_recv()
        relay(source, h, h_core, s3, r3).start()

    def pass_second(source):
        relay(source, h_x, h_x, s2, r2).wait_recv()
        relay(source, h_x, h_core, s4, r4).start()

    def complete(source):
        relay(source, h_core, h_core, s3, r3).wait_recv()
        relay(source, h_diag, h_core, s4, r4).wait_recv()

    def same(step):
        return 2 * (plane - 1 - step) + side

    def other(step):
        return 2 * (plane - step) + (1 - side)

    def has_same(step):
        return (step >= 0) & (step < plane)

    def has_other(step):
        return (step >= 1 - side) & (step <= plane)

    @pl.loop(0, plane + 3)
    def _(step):
        @pl.when(has_same(step))
        def _():
            source = same(step)
            first_copy(source, c).wait_recv()
            side_copy(source, h, 0, r1).start()
            side_copy(source, h_x, 1, r2).start()
            relay(source, h, h_x, s2, r2).start()
            relay(source, h, h_core, s3, r3).start()

        @pl.when(step == plane)
        def _():
            build_queries()

        @pl.when(has_other(step - 1))
        def _():
            pass_first(other(step - 1))
            pass_second(other(step - 1))

        @pl.when(has_same(step - 2))
        def _():
            pass_second(same(step - 2))

        @pl.when(has_other(step - 2))
        def _():
            complete(other(step - 2))

        @pl.when(has_same(step - 3))
        def _():
            complete(same(step - 3))

    load_w.wait()
    load_sel.wait()

    factor = (DV + DR) ** (-0.5) * math.log2(math.e)
    key_row = lax.broadcasted_iota(jnp.int32, (SEL * KBLK, 1), 0)
    width = per_group * DV
    token = lax.broadcasted_iota(jnp.int32, (1, columns), 1) % KBLK

    def out_copy(group, target, relation):
        return pltpu.make_async_remote_copy(
            src_ref=stage.at[target, :, pl.ds(group * width, width)],
            dst_ref=out_ref.at[:, pl.ds(pl.multiple_of(h * (heads * DV) + group * width, width), width)],
            send_sem=s_out.at[relation, group], recv_sem=r_out.at[relation, group],
            device_id=(c, target), device_id_type=MESH,
        )

    def out_local(group):
        return pltpu.make_async_copy(
            stage.at[h, :, pl.ds(group * width, width)],
            out_ref.at[:, pl.ds(pl.multiple_of(h * (heads * DV) + group * width, width), width)],
            l_out.at[group],
        )

    half = KBLK // 2

    def slots_of(position):
        chosen = [sel_ref[position, slot] for slot in range(SEL)]
        return chosen, [jnp.maximum(one, 0) for one in chosen]

    def weigh(turn, position, group):
        chosen, _ = slots_of(position)
        key_block = jnp.full((SEL * KBLK, 1), chosen[0], jnp.int32)
        for slot in range(1, SEL):
            key_block = jnp.where(key_row // KBLK == slot, chosen[slot], key_block)
        key_place = jnp.where(key_block < 0, FAR, key_block * KBLK + key_row % KBLK)
        query_place = token + (c * blocks + position) * KBLK
        scores = jnp.dot(kbuf[turn], q_blocks[position, group], preferred_element_type=jnp.float32)
        scores = jnp.where(key_place <= query_place, scores, -1e30)
        largest = jnp.max(scores, axis=0, keepdims=True)
        powered = jnp.exp2((scores - largest) * factor)
        total = jnp.sum(powered, axis=0, keepdims=True)
        return (powered * (1.0 / total)).astype(jnp.bfloat16).T

    def finish(turn, position, group, weights):
        latent = jnp.dot(weights, kbuf[turn, :, :DC], preferred_element_type=jnp.float32).astype(jnp.bfloat16)
        for inner in range(per_group):
            head = group * per_group + inner
            value = jnp.dot(
                latent[inner * KBLK:(inner + 1) * KBLK], w_ref[head], preferred_element_type=jnp.float32
            ).astype(jnp.bfloat16)
            stage[2 * position, :, head * DV:(head + 1) * DV] = value[:half]
            stage[2 * position + 1, :, head * DV:(head + 1) * DV] = value[half:]

    def send(turn, group):
        if turn == 0:
            out_copy(group, h_x, 0).start()
            out_copy(group, h_diag, 1).start()
        else:
            out_copy(group, h_core, 2).start()
            out_local(group).start()

    order = [(turn, (1 - x) if turn == 0 else x, group) for turn in range(2) for group in range(GROUPS)]
    for turn in range(2):
        _, entry = slots_of((1 - x) if turn == 0 else x)
        for slot in range(SEL):
            kbuf[turn, slot * KBLK:(slot + 1) * KBLK, :] = keys[entry[slot]]
    weights = weigh(*order[0])
    for number, (turn, position, group) in enumerate(order):
        after = None
        if number + 1 < len(order):
            after = weigh(*order[number + 1])
        finish(turn, position, group, weights)
        send(turn, group)
        weights = after

    for group in range(GROUPS):
        out_local(group).wait()
        for relation, peer in enumerate((h_x, h_diag, h_core)):
            out_copy(group, peer, relation).wait()

    @pl.when(side == 0)
    def _():
        pair_copy(c, h, 0, r1).wait_send()
        pair_copy(c, h_x, 1, r2).wait_send()

    @pl.loop(0, above)
    def _(step):
        first_copy(c, n_ctx - 2 + side - 2 * step).wait_send()

    @pl.loop(0, c)
    def _(source):
        relay(source, h, h_core, s3, r3).wait_send()
        relay(source, h_x, h_core, s4, r4).wait_send()

    @pl.loop(0, plane)
    def _(lower):
        source = 2 * lower + side
        relay(source, h, h_x, s2, r2).wait_send()
        side_copy(source, h, 0, r1).wait_send()
        side_copy(source, h_x, 1, r2).wait_send()


def per_device(queries, latent_cache, selected, value_weight):
    n_ctx, n_head = lax.axis_size("ctx"), lax.axis_size("head")
    width = DC + DR
    tokens, heads = queries.shape[:2]
    own = latent_cache.reshape(tokens, width)
    by_head = queries.transpose(1, 2, 0)
    part = tokens // n_head
    dma = pltpu.SemaphoreType.DMA
    return pl.pallas_call(
        functools.partial(kernel, n_ctx, n_head, heads),
        out_shape=jax.ShapeDtypeStruct((part, n_head * heads * DV), jnp.bfloat16),
        in_specs=[
            pl.BlockSpec(memory_space=pltpu.HBM),
            pl.BlockSpec(memory_space=pltpu.VMEM),
            pl.BlockSpec(memory_space=pl.ANY),
            pl.BlockSpec(memory_space=pl.ANY),
        ],
        out_specs=pl.BlockSpec(memory_space=pl.ANY),
        scratch_shapes=[
            pltpu.SMEM(selected.shape, jnp.int32),
            pltpu.VMEM((n_ctx * tokens // KBLK, KBLK, width), jnp.bfloat16),
            pltpu.VMEM((2, SEL * KBLK, width), jnp.bfloat16),
            pltpu.VMEM((heads, width, tokens), jnp.bfloat16),
            pltpu.VMEM((tokens // KBLK, GROUPS, width, heads // GROUPS * KBLK), jnp.bfloat16),
            pltpu.VMEM((heads, DC, DV), jnp.bfloat16),
            pltpu.VMEM((n_head, part, heads * DV), jnp.bfloat16),
            dma((3,)), dma((2,)), dma((2, n_ctx)),
            dma((n_ctx,)), dma((n_ctx,)),
            dma((n_ctx,)), dma((n_ctx,)),
            dma((n_ctx,)), dma((n_ctx,)),
            dma((n_ctx,)), dma((n_ctx,)),
            dma((3, GROUPS)), dma((3, GROUPS)), dma((GROUPS,)),
        ],
        compiler_params=pltpu.CompilerParams(
            collective_id=0, has_side_effects=True, vmem_limit_bytes=VMEM_LIMIT
        ),
    )(selected, own, by_head, value_weight)


def solution(mesh):
    in_specs = (P("ctx", "head", None), P("ctx", None), P("ctx", None), P("head", None, None))
    out_specs = P(("ctx", "head"), None)
    return jax.shard_map(
        per_device, mesh=mesh, in_specs=in_specs, out_specs=out_specs, check_vma=False
    )
```

```python
import functools
import math

import jax
import jax.numpy as jnp
from jax import lax
from jax.experimental import pallas as pl
from jax.experimental.pallas import tpu as pltpu
from jax.sharding import PartitionSpec as P

DC = 512
DR = 64
DV = 128
KBLK = 64
SEL = 8
GROUPS = 8
MESH = pl.DeviceIdType.MESH
FAR = 1 << 30
VMEM_LIMIT = 52 * 1024 * 1024


def kernel(
    n_ctx, n_head, heads,
    sel_hbm, own_ref, q_hbm, w_hbm, out_ref,
    sel_ref, keys, kbuf, q_ref, q_blocks, w_ref, stage,
    load_sem, s_pair, s_side, s1, r1, s2, r2, s3, r3, s4, r4, s_out, r_out, l_out,
):
    c = lax.axis_index("ctx")
    h = lax.axis_index("head")
    plane, side = c // 2, c % 2
    c_pair = 2 * plane + (1 - side)
    x, core = h // 2, h % 2
    h_core = 2 * x + (1 - core)
    h_x = 2 * (1 - x) + core
    h_diag = 2 * (1 - x) + (1 - core)
    own_rows = own_ref.shape[0]
    blocks = own_rows // KBLK
    part = own_rows // n_head

    load_q = pltpu.make_async_copy(q_hbm, q_ref, load_sem.at[0])
    load_w = pltpu.make_async_copy(w_hbm, w_ref, load_sem.at[1])
    load_sel = pltpu.make_async_copy(sel_hbm, sel_ref, load_sem.at[2])
    load_q.start()
    load_sel.start()
    load_w.start()

    barrier = pltpu.get_barrier_semaphore()
    for peer in (h_core, h_x, h_diag):
        pl.semaphore_signal(barrier, inc=1, device_id=(c, peer), device_id_type=MESH)

    for peer in (h, h_x):
        pl.semaphore_signal(barrier, inc=1, device_id=(c_pair, peer), device_id_type=MESH)

    @pl.loop(0, plane)
    def _(lower):
        pl.semaphore_signal(barrier, inc=1, device_id=(2 * lower + side, h), device_id_type=MESH)

    above = n_ctx // 2 - 1 - plane
    pl.semaphore_wait(barrier, 5 + above)

    def piece(source, quarter):
        row = quarter * part
        start = pl.multiple_of(row % KBLK, part)
        return keys.at[source * blocks + row // KBLK, pl.ds(start, part), :]

    def first_copy(source, target):
        return pltpu.make_async_remote_copy(
            src_ref=own_ref.at[pl.ds(pl.multiple_of(h * part, part), part), :],
            dst_ref=piece(source, h),
            send_sem=s1.at[target], recv_sem=r1.at[source],
            device_id=(target, h), device_id_type=MESH,
        )

    def pair_copy(source, quarter, send, recv):
        return pltpu.make_async_remote_copy(
            src_ref=own_ref.at[pl.ds(pl.multiple_of(quarter * part, part), part), :],
            dst_ref=piece(source, quarter),
            send_sem=s_pair.at[send], recv_sem=recv.at[source],
            device_id=(c_pair, h), device_id_type=MESH,
        )

    def side_copy(source, peer, send, recv):
        return pltpu.make_async_remote_copy(
            src_ref=piece(source, h), dst_ref=piece(source, h),
            send_sem=s_side.at[send, source], recv_sem=recv.at[source],
            device_id=(c_pair, peer), device_id_type=MESH,
        )

    def relay(source, quarter, peer, send, recv):
        return pltpu.make_async_remote_copy(
            src_ref=piece(source, quarter), dst_ref=piece(source, quarter),
            send_sem=send.at[source], recv_sem=recv.at[source],
            device_id=(c, peer), device_id_type=MESH,
        )

    @pl.loop(0, above)
    def _(step):
        first_copy(c, n_ctx - 2 + side - 2 * step).start()

    @pl.when(side == 0)
    def _():
        pair_copy(c, h, 0, r1).start()
        pair_copy(c, h_x, 1, r2).start()

    for block in range(blocks):
        keys[c * blocks + block] = own_ref[block * KBLK:(block + 1) * KBLK, :]

    per_group = heads // GROUPS
    columns = per_group * KBLK

    def build_queries():
        load_q.wait()
        for pair in range(heads // 2):
            group, slot = divmod(pair, heads // (2 * GROUPS))
            lanes = slice(slot * 2 * KBLK, (slot + 1) * 2 * KBLK)
            first, second = q_ref[2 * pair], q_ref[2 * pair + 1]
            q_blocks[0, group, :, lanes] = jnp.concatenate([first[:, :KBLK], second[:, :KBLK]], axis=1)
            q_blocks[1, group, :, lanes] = jnp.concatenate([first[:, KBLK:], second[:, KBLK:]], axis=1)

    def pass_first(source):
        first_copy(source, c).wait_recv()
        relay(source, h, h_core, s3, r3).start()

    def pass_second(source):
        relay(source, h_x, h_x, s2, r2).wait_recv()
        relay(source, h_x, h_core, s4, r4).start()

    def complete(source):
        relay(source, h_core, h_core, s3, r3).wait_recv()
        relay(source, h_diag, h_core, s4, r4).wait_recv()

    def same(step):
        return 2 * (plane - 1 - step) + side

    def other(step):
        return 2 * (plane - step) + (1 - side)

    def has_same(step):
        return (step >= 0) & (step < plane)

    def has_other(step):
        return (step >= 1 - side) & (step <= plane)

    @pl.loop(0, plane + 3)
    def _(step):
        @pl.when(has_same(step))
        def _():
            source = same(step)
            first_copy(source, c).wait_recv()
            side_copy(source, h, 0, r1).start()
            side_copy(source, h_x, 1, r2).start()
            relay(source, h, h_x, s2, r2).start()
            relay(source, h, h_core, s3, r3).start()

        @pl.when(step == plane)
        def _():
            build_queries()

        @pl.when(has_other(step - 1))
        def _():
            pass_first(other(step - 1))
            pass_second(other(step - 1))

        @pl.when(has_same(step - 2))
        def _():
            pass_second(same(step - 2))

        @pl.when(has_other(step - 2))
        def _():
            complete(other(step - 2))

        @pl.when(has_same(step - 3))
        def _():
            complete(same(step - 3))

    load_w.wait()
    load_sel.wait()

    factor = (DV + DR) ** (-0.5) * math.log2(math.e)
    key_row = lax.broadcasted_iota(jnp.int32, (SEL * KBLK, 1), 0)
    width = per_group * DV
    token = lax.broadcasted_iota(jnp.int32, (1, columns), 1) % KBLK

    def out_copy(group, target, relation):
        return pltpu.make_async_remote_copy(
            src_ref=stage.at[target, :, pl.ds(group * width, width)],
            dst_ref=out_ref.at[:, pl.ds(pl.multiple_of(h * (heads * DV) + group * width, width), width)],
            send_sem=s_out.at[relation, group], recv_sem=r_out.at[relation, group],
            device_id=(c, target), device_id_type=MESH,
        )

    def out_local(group):
        return pltpu.make_async_copy(
            stage.at[h, :, pl.ds(group * width, width)],
            out_ref.at[:, pl.ds(pl.multiple_of(h * (heads * DV) + group * width, width), width)],
            l_out.at[group],
        )

    half = KBLK // 2

    def slots_of(position):
        chosen = [sel_ref[position, slot] for slot in range(SEL)]
        return chosen, [jnp.maximum(one, 0) for one in chosen]

    def weigh(turn, position, group):
        chosen, _ = slots_of(position)
        key_block = jnp.full((SEL * KBLK, 1), chosen[0], jnp.int32)
        for slot in range(1, SEL):
            key_block = jnp.where(key_row // KBLK == slot, chosen[slot], key_block)
        key_place = jnp.where(key_block < 0, FAR, key_block * KBLK + key_row % KBLK)
        query_place = token + (c * blocks + position) * KBLK
        scores = jnp.dot(kbuf[turn], q_blocks[position, group], preferred_element_type=jnp.float32)
        scores = jnp.where(key_place <= query_place, scores, -1e30)
        largest = jnp.max(scores, axis=0, keepdims=True)
        powered = jnp.exp2((scores - largest) * factor)
        total = jnp.sum(powered, axis=0, keepdims=True)
        return (powered * (1.0 / total)).astype(jnp.bfloat16).T

    def finish(turn, position, group, weights):
        latent = jnp.dot(weights, kbuf[turn, :, :DC], preferred_element_type=jnp.float32).astype(jnp.bfloat16)
        for inner in range(per_group):
            head = group * per_group + inner
            value = jnp.dot(
                latent[inner * KBLK:(inner + 1) * KBLK], w_ref[head], preferred_element_type=jnp.float32
            ).astype(jnp.bfloat16)
            stage[2 * position, :, head * DV:(head + 1) * DV] = value[:half]
            stage[2 * position + 1, :, head * DV:(head + 1) * DV] = value[half:]

    def send(turn, group):
        if turn == 0:
            out_copy(group, h_x, 0).start()
            out_copy(group, h_diag, 1).start()
        else:
            out_copy(group, h_core, 2).start()
            out_local(group).start()

    order = [(turn, (1 - x) if turn == 0 else x, group) for turn in range(2) for group in range(GROUPS)]
    for turn in range(2):
        _, entry = slots_of((1 - x) if turn == 0 else x)
        for slot in range(SEL):
            kbuf[turn, slot * KBLK:(slot + 1) * KBLK, :] = keys[entry[slot]]
    weights = weigh(*order[0])
    for number, (turn, position, group) in enumerate(order):
        after = None
        if number + 1 < len(order):
            after = weigh(*order[number + 1])
        finish(turn, position, group, weights)
        send(turn, group)
        weights = after

    for group in range(GROUPS):
        out_local(group).wait()
        for relation, peer in enumerate((h_x, h_diag, h_core)):
            out_copy(group, peer, relation).wait()

    @pl.when(side == 0)
    def _():
        pair_copy(c, h, 0, r1).wait_send()
        pair_copy(c, h_x, 1, r2).wait_send()

    @pl.loop(0, above)
    def _(step):
        first_copy(c, n_ctx - 2 + side - 2 * step).wait_send()

    @pl.loop(0, c)
    def _(source):
        relay(source, h, h_core, s3, r3).wait_send()
        relay(source, h_x, h_core, s4, r4).wait_send()

    @pl.loop(0, plane)
    def _(lower):
        source = 2 * lower + side
        relay(source, h, h_x, s2, r2).wait_send()
        side_copy(source, h, 0, r1).wait_send()
        side_copy(source, h_x, 1, r2).wait_send()


def per_device(queries, latent_cache, selected, value_weight):
    n_ctx, n_head = lax.axis_size("ctx"), lax.axis_size("head")
    width = DC + DR
    tokens, heads = queries.shape[:2]
    own = latent_cache.reshape(tokens, width)
    by_head = queries.transpose(1, 2, 0)
    part = tokens // n_head
    dma = pltpu.SemaphoreType.DMA
    return pl.pallas_call(
        functools.partial(kernel, n_ctx, n_head, heads),
        out_shape=jax.ShapeDtypeStruct((part, n_head * heads * DV), jnp.bfloat16),
        in_specs=[
            pl.BlockSpec(memory_space=pltpu.HBM),
            pl.BlockSpec(memory_space=pltpu.VMEM),
            pl.BlockSpec(memory_space=pl.ANY),
            pl.BlockSpec(memory_space=pl.ANY),
        ],
        out_specs=pl.BlockSpec(memory_space=pl.ANY),
        scratch_shapes=[
            pltpu.SMEM(selected.shape, jnp.int32),
            pltpu.VMEM((n_ctx * tokens // KBLK, KBLK, width), jnp.bfloat16),
            pltpu.VMEM((2, SEL * KBLK, width), jnp.bfloat16),
            pltpu.VMEM((heads, width, tokens), jnp.bfloat16),
            pltpu.VMEM((tokens // KBLK, GROUPS, width, heads // GROUPS * KBLK), jnp.bfloat16),
            pltpu.VMEM((heads, DC, DV), jnp.bfloat16),
            pltpu.VMEM((n_head, part, heads * DV), jnp.bfloat16),
            dma((3,)), dma((2,)), dma((2, n_ctx)),
            dma((n_ctx,)), dma((n_ctx,)),
            dma((n_ctx,)), dma((n_ctx,)),
            dma((n_ctx,)), dma((n_ctx,)),
            dma((n_ctx,)), dma((n_ctx,)),
            dma((3, GROUPS)), dma((3, GROUPS)), dma((GROUPS,)),
        ],
        compiler_params=pltpu.CompilerParams(
            collective_id=0, has_side_effects=True, vmem_limit_bytes=VMEM_LIMIT
        ),
    )(selected, own, by_head, value_weight)


def solution(mesh):
    in_specs = (P("ctx", "head", None), P("ctx", None), P("ctx", None), P("head", None, None))
    out_specs = P(("ctx", "head"), None)
    return jax.shard_map(
        per_device, mesh=mesh, in_specs=in_specs, out_specs=out_specs, check_vma=False
    )
```
